128 devices in a mesh: grp: 8 (over y, core), seq: 16 (over x, z).
Axes of the slice: x: 4, y: 4, z: 4, core: 2. Of those that a mesh axis runs over, the one named last changes fastest.
Arguments:
- prefill_cache: bfloat16 [128, 16384, 576], P('grp', 'seq'), may hold values from -9 to 9
- lengths: int32 [128], replicated, may hold values from 2 to 16384, as said below
- decode_slots: int32 [8, 16], replicated, may hold values from 0 to 127, as said below
- q_nope: bfloat16 [2, 128, 16384], P(None, 'grp', 'seq'), may hold values from -6 to 6
- q_pe: bfloat16 [2, 128, 8192], P(None, 'grp', 'seq'), may hold values from -8 to 8
- new_latent: bfloat16 [2, 128, 576], P(None, 'grp'), may hold values from -6 to 6
- w_uk: bfloat16 [128, 128, 512], P('seq'), may hold values from -0.5 to 0.5
- value_up_weight: bfloat16 [128, 512, 128], P('seq'), may hold values from -0.25 to 0.25
Outputs:
- attended: bfloat16 [2, 128, 16384], P(None, 'grp', 'seq')
The draws below stay inside these ranges and needn't reach their ends.
Inputs may be any that keep to these rules, and one draw needn't show every extreme that they name: `decode_slots`: every request id appears exactly once. Of the 16 requests of one row, at most 3 lie in one aligned run of 16 request ids; every run has 3 requests in some row. `lengths`: some request has exactly 16384 rows.
All inputs are finite; a program needn't handle non-finite values.
Results may differ from the reference program's by a relative error of at most 0.018.
Values may be sent and summed in bfloat16 or wider, within the bound.
A program may use at most 192 MiB of HBM per device.

```python
import jax
import jax.numpy as jnp
from jax import lax

HEADS = 128
KVL = 512
ROPE = 64
NOPE = 128
VD = 128
REQ = 16
CTX = 16384
STEPS = 2
REQS = 128
BLK = 1024
CAP = 3
N_GRP = 8
N_SEQ = 16


def draw_prefill_cache(key, part):
    key = jax.random.fold_in(key, 3)
    base_key = jax.random.fold_in(key, 0)
    values = jnp.clip(jax.random.normal(base_key, (REQS, CTX, KVL + ROPE), jnp.float32), -6.0, 6.0)
    return values.astype(jnp.bfloat16)


def draw_q_pe(key, part):
    key = jax.random.fold_in(key, 4)
    base_key = jax.random.fold_in(key, 0)
    values = jnp.clip(jax.random.normal(base_key, (STEPS, REQS, HEADS, ROPE), jnp.float32), -6.0, 6.0)
    return values.reshape(STEPS, REQS, HEADS * ROPE).astype(jnp.bfloat16)


def draw_lengths(key, part):
    key = jax.random.fold_in(key, 2)
    length_key, index_key = jax.random.split(key)
    values = jax.random.randint(length_key, (REQS,), 2, CTX + 1, jnp.int32)
    longest = jax.random.randint(index_key, (), 0, REQS, jnp.int32)
    return values.at[longest].set(CTX)


def draw_decode_slots(key, part):
    key = jax.random.fold_in(key, 1)
    offset_key, perm_key, ordering_random_key = jax.random.split(key, 3)
    offset = jax.random.randint(offset_key, (), 0, N_GRP, jnp.int32)
    bins = jnp.arange(N_GRP, dtype=jnp.int32)
    counts = jnp.where(bins == 0, CAP, jnp.where(bins == 1, REQ // (2 * N_GRP), REQ // N_GRP)).astype(jnp.int32)
    bounds = jnp.cumsum(counts)
    group_keys = jax.random.split(perm_key, N_GRP)
    shuffled = jax.vmap(lambda one_key: jax.random.permutation(one_key, REQ))(group_keys).astype(jnp.int32)
    which_bin = jnp.sum((shuffled[:, :, None] >= bounds[None, None, :]).astype(jnp.int32), axis=2)
    prefill_group = jnp.arange(N_GRP, dtype=jnp.int32)[:, None]
    destination = ((prefill_group + which_bin + offset) % N_GRP).reshape(-1)
    ranks = jax.random.permutation(ordering_random_key, REQS).astype(jnp.int32)
    sort_keys = destination * REQS + ranks
    order = jnp.argsort(sort_keys, stable=True).astype(jnp.int32)
    return order.reshape(N_GRP, REQ)


def shard_levels(own_key, shape, shards, low, top_value):
    gain, own = 1.0, jax.random.fold_in(own_key, 6)
    for position, blocks in shards:
        heights = jnp.exp(jax.random.uniform(jax.random.fold_in(own, position), (blocks,), jnp.float32, low / len(shards), top_value / len(shards)))
        gain = gain * jnp.repeat(heights, shape[position] // blocks).reshape([-1 if axis == position else 1 for axis in range(len(shape))])
    return gain


def scatter_about(stream_key, dims, spread, limit, cuts=(), held_as=jnp.bfloat16):
    entries = jax.random.normal(stream_key, dims, jnp.float32) * spread
    if len(cuts) > 0:
        entries = shard_levels(stream_key, dims, cuts, -0.22, 0.18) * entries
    return jnp.clip(entries, min=-limit, max=limit).astype(held_as)


def setup_inputs(seed: int = 0) -> dict:
    key_of = jax.random.split(jax.random.key(seed), 9)
    return {
        "prefill_cache": draw_prefill_cache(jax.random.fold_in(key_of[8], 71), 0),
        "lengths": draw_lengths(jax.random.fold_in(key_of[8], 71), 0),
        "decode_slots": draw_decode_slots(jax.random.fold_in(key_of[8], 71), 0),
        "q_nope": scatter_about(key_of[3], (STEPS, REQS, HEADS * NOPE), 1.0, 6.0, ((1, 8), (2, 16))),
        "q_pe": draw_q_pe(jax.random.fold_in(key_of[8], 71), 0),
        "new_latent": scatter_about(key_of[5], (STEPS, REQS, KVL + ROPE), 1.0, 6.0, ((1, 8),)),
        "w_uk": scatter_about(key_of[6], (HEADS, NOPE, KVL), NOPE ** -0.5, 0.5, ((0, 16),)),
        "value_up_weight": scatter_about(key_of[7], (HEADS, KVL, VD), KVL ** -0.5, 0.25, ((0, 16),)),
    }


def slot_attention(cache_rows, length, query_rows, fresh_rows, value_up_weight):
    score_scale = (NOPE + ROPE) ** -0.5
    scores = jnp.dot(query_rows, cache_rows.T, preferred_element_type=jnp.float32) * score_scale
    in_range = jnp.arange(CTX, dtype=jnp.int32) < length
    fresh_scores = jnp.dot(query_rows, fresh_rows.T, preferred_element_type=jnp.float32) * score_scale
    query_step = jnp.arange(STEPS * HEADS, dtype=jnp.int32) // HEADS
    fresh_mask = jnp.arange(STEPS, dtype=jnp.int32)[None, :] <= query_step[:, None]
    cache_high = jnp.max(jnp.where(in_range[None, :], scores, -1e30), axis=1)
    fresh_high = jnp.max(jnp.where(fresh_mask, fresh_scores, -1e30), axis=1)
    highest = jnp.maximum(cache_high, fresh_high)
    weights = jnp.where(in_range[None, :], jnp.exp(scores - highest[:, None]), 0.0)
    shard_weights = weights.astype(jnp.bfloat16).reshape(STEPS * HEADS, N_SEQ, BLK).astype(jnp.float32)
    shard_values = cache_rows[:, :KVL].reshape(N_SEQ, BLK, KVL).astype(jnp.float32)
    part_num = jnp.einsum("qjp,jpk->jqk", shard_weights, shard_values).astype(jnp.bfloat16)
    part_num = lax.optimization_barrier(part_num).astype(jnp.float32)
    part_den = jnp.sum(weights.reshape(STEPS * HEADS, N_SEQ, BLK), axis=2).astype(jnp.bfloat16)
    part_den = lax.optimization_barrier(part_den).astype(jnp.float32)
    fresh_weights = jnp.where(fresh_mask, jnp.exp(fresh_scores - highest[:, None]), 0.0)
    numerator = jnp.sum(part_num, axis=0) + jnp.dot(fresh_weights.astype(jnp.bfloat16), fresh_rows[:, :KVL], preferred_element_type=jnp.float32)
    denominator = jnp.sum(part_den, axis=1) + jnp.sum(fresh_weights, axis=1)
    latent_output = (numerator / denominator[:, None]).astype(jnp.bfloat16).reshape(STEPS, HEADS, KVL)
    value_projected = jnp.einsum("wnf,nfj->wnj", latent_output.astype(jnp.float32), value_up_weight.astype(jnp.float32))
    return value_projected.astype(jnp.bfloat16)


def reference(prefill_cache, lengths, decode_slots, q_nope, q_pe, new_latent, w_uk, value_up_weight):
    nope_parts = q_nope.reshape(STEPS, REQS, HEADS, NOPE).astype(jnp.float32)
    absorbed = jnp.einsum("trhn,hnk->trhk", nope_parts, w_uk.astype(jnp.float32)).astype(jnp.bfloat16)
    rope_parts = q_pe.reshape(STEPS, REQS, HEADS, ROPE)
    queries = jnp.concatenate([absorbed, rope_parts], axis=3)
    queries = queries.transpose(1, 0, 2, 3).reshape(REQS, STEPS * HEADS, KVL + ROPE)
    served = decode_slots.reshape(-1)
    fresh_all = new_latent.transpose(1, 0, 2)

    def one_slot(index):
        request = served[index]
        return slot_attention(prefill_cache[request], lengths[request], queries[index], fresh_all[index], value_up_weight)

    attended = lax.map(one_slot, jnp.arange(REQS, dtype=jnp.int32))
    return attended.transpose(1, 0, 2, 3).reshape(STEPS, REQS, HEADS * VD)
```

```python
import functools

import jax
import jax.numpy as jnp
from jax import lax
from jax.experimental import pallas as pl
from jax.experimental.pallas import tpu as pltpu
from jax.sharding import PartitionSpec as P

MESH = pl.DeviceIdType.MESH
LOG2E = 1.4426950408889634
LOW = -1e30
CAP = 3
NX = 4
NZ = 4
F32 = jnp.float32
BF16 = jnp.bfloat16


def dot(a, b):
    return jnp.dot(a, b, preferred_element_type=F32)


def dot_nt(a, b):
    return lax.dot_general(a, b, (((1,), (1,)), ((), ())), preferred_element_type=F32)


def iota(shape, dim):
    return lax.broadcasted_iota(jnp.int32, shape, dim)


def pick(cond):
    return jnp.where(cond, 1.0, 0.0).astype(BF16)


def kernel(
    ngrp, nreq, blk, scale2,
    lens, rho_row, rho_col, sig_row, sig_col, qn, qp, lat, w_uk, w_v, cache,
    out,
    cbuf, tx, rx, latrep, qall, pout, stat, r1, st1, red1, stat2, r2, st2, fin, flse, tx2, rx2,
    c_sem, rt_s, rt_r, g1_s, g1_r, g2_s, g2_r, s1_s, s1_r, t1_s, t1_r, s2_s, s2_r, t2_s, t2_r,
    rb_s, rb_r,
):
    g = lax.axis_index("grp")
    s = lax.axis_index("seq")
    x = lax.div(s, NZ)
    z = lax.rem(s, NZ)
    half = nreq // 2
    rows = nreq * 16
    lw = 512
    c_copies = [pltpu.make_async_copy(cache.at[r], cbuf.at[r], c_sem.at[r]) for r in range(nreq)]
    for c in c_copies:
        c.start()

    def gid(k):
        return {"grp": lax.rem(g + k, ngrp)}

    def xid(k):
        return {"seq": lax.rem(x + k, NX) * NZ + z}

    def zid(k):
        return {"seq": x * NZ + lax.rem(z + k, NZ)}

    def rcopy(src, dst, ss, rs, dev):
        return pltpu.make_async_remote_copy(
            src_ref=src, dst_ref=dst, send_sem=ss, recv_sem=rs, device_id=dev, device_id_type=MESH
        )

    barrier = pltpu.get_barrier_semaphore()
    for k in range(1, ngrp):
        pl.semaphore_signal(barrier, inc=1, device_id=gid(k), device_id_type=MESH)
    for k in range(1, 4):
        pl.semaphore_signal(barrier, inc=1, device_id=xid(k), device_id_type=MESH)
        pl.semaphore_signal(barrier, inc=1, device_id=zid(k), device_id_type=MESH)

    bl = ngrp * 16
    row_l = iota((bl, 2 * nreq), 0)
    s0 = pick(row_l == rho_row[...])
    s1 = pick(row_l == rho_row[...] + 2 * CAP)
    head = dot(s0, qn[:, :lw]) + dot(s1, qp[...])
    tx[:, :, :lw] = head.astype(BF16).reshape(ngrp, 16, lw)
    mid = dot(s0, qn[:, lw:]) + dot(s1, lat[:, :lw])
    tx[:, :, lw : 2 * lw] = mid.astype(BF16).reshape(ngrp, 16, lw)
    tx[:, :, 2 * lw :] = dot(s1, lat[:, lw:]).astype(BF16).reshape(ngrp, 16, 64)
    stat[...] = jnp.zeros_like(stat)

    pl.semaphore_wait(barrier, ngrp - 1 + 6)
    route = [
        rcopy(tx.at[lax.rem(g + k, ngrp)], rx.at[g], rt_s.at[k], rt_r.at[k], gid(k))
        for k in range(1, ngrp)
    ]
    for c in route:
        c.start()
    rx[g] = tx[g]
    for k in range(1, ngrp):
        src = lax.rem(g + ngrp - k, ngrp)
        rcopy(tx.at[src], rx.at[src], rt_s.at[k], rt_r.at[k], gid(k)).wait_recv()

    col_l = iota((rows, bl), 1)
    m0 = pick(col_l == sig_col[...])
    m1 = pick(col_l == sig_col[...] + 2 * CAP)
    own = iota((rows, lw), 0) % 8
    lane = iota((rows, lw), 1)
    absorbed = jnp.zeros((rows, lw), F32)
    for j in range(2):
        spread = dot(m0, rx[:, :, j * lw : (j + 1) * lw].reshape(bl, lw))
        spread = jnp.where(lane // 128 + 4 * j == own, spread, 0.0).astype(BF16)
        absorbed += dot(spread, w_uk[j * lw : (j + 1) * lw, :])
    qall[:, x, z, :, :lw] = absorbed.astype(BF16).reshape(nreq, 16, lw)
    spread = dot(m1, rx[:, :, :lw].reshape(bl, lw))
    spread = jnp.where(lane // 64 == own, spread, 0.0).astype(BF16)
    fold = pick(iota((lw, 64), 0) % 64 == iota((lw, 64), 1))
    qall[:, x, z, :, lw:] = dot(spread, fold).astype(BF16).reshape(nreq, 16, 64)

    lo = pl.ds(0, half)
    hi = pl.ds(half, half)
    mine_a = qall.at[lo, x, z]
    mine_b = qall.at[hi, x, z]
    gather1 = []
    for k in (1, 3, 2):
        gather1.append(rcopy(mine_a, mine_a, g1_s.at[0, k], g1_r.at[0, k], zid(k)))
        gather1.append(rcopy(mine_b, mine_b, g1_s.at[1, k], g1_r.at[1, k], xid(k)))
    for c in gather1:
        c.start()
    latrep[:, :lw] = dot(m1, rx[:, :, lw : 2 * lw].reshape(bl, lw)).astype(BF16)
    latrep[:, lw:] = dot(m1, rx[:, :, 2 * lw :].reshape(bl, 64)).astype(BF16)
    for k in (1, 3, 2):
        za = qall.at[lo, x, lax.rem(z + 4 - k, NZ)]
        xb = qall.at[hi, lax.rem(x + 4 - k, NX), z]
        rcopy(za, za, g1_s.at[0, k], g1_r.at[0, k], zid(k)).wait_recv()
        rcopy(xb, xb, g1_s.at[1, k], g1_r.at[1, k], xid(k)).wait_recv()

    xl = lax.rem(x + 3, NX)
    xr = lax.rem(x + 1, NX)
    xo = lax.rem(x + 2, NX)
    zl = lax.rem(z + 3, NZ)
    zr = lax.rem(z + 1, NZ)
    zo = lax.rem(z + 2, NZ)
    two = (pl.ds(0, 2), pl.ds(2, 2))

    def wide(i, part, ref, j, dev):
        return rcopy(ref, ref, g2_s.at[part, j, i], g2_r.at[part, j, i], dev)

    def direct(i):
        a = qall.at[i, x]
        b = qall.at[half + i, :, z]
        return [
            wide(i, 0, a, 0, xid(1)), wide(i, 1, b, 0, zid(1)),
            wide(i, 0, a, 1, xid(3)), wide(i, 1, b, 1, zid(3)),
        ]

    def direct_in(i):
        return [
            wide(i, 0, qall.at[i, xl], 0, xid(1)), wide(i, 1, qall.at[half + i, :, zl], 0, zid(1)),
            wide(i, 0, qall.at[i, xr], 1, xid(3)), wide(i, 1, qall.at[half + i, :, zr], 1, zid(3)),
        ]

    def onward(i):
        return [
            wide(i, 0, qall.at[i, xl, two[0]], 2, xid(1)),
            wide(i, 1, qall.at[half + i, two[0], zl], 2, zid(1)),
            wide(i, 0, qall.at[i, xr, two[1]], 3, xid(3)),
            wide(i, 1, qall.at[half + i, two[1], zr], 3, zid(3)),
        ]

    def onward_in(i):
        return [
            wide(i, 0, qall.at[i, xo, two[0]], 2, xid(1)),
            wide(i, 1, qall.at[half + i, two[0], zo], 2, zid(1)),
            wide(i, 0, qall.at[i, xo, two[1]], 3, xid(3)),
            wide(i, 1, qall.at[half + i, two[1], zo], 3, zid(3)),
        ]

    def start(copies):
        for c in copies:
            c.start()

    def relay(i):
        for c, f in zip(direct_in(i), onward(i)):
            c.wait_recv()
            f.start()

    def scatter1(i):
        out_copies = []
        for k in (1, 3, 2):
            out_copies.append(
                rcopy(pout.at[i, lax.rem(x + k, NX)], r1.at[0, k - 1, i],
                      s1_s.at[0, k - 1, i], s1_r.at[0, k - 1, i], xid(k))
            )
            out_copies.append(
                rcopy(pout.at[half + i, :, lax.rem(z + k, NZ)], r1.at[1, k - 1, i],
                      s1_s.at[1, k - 1, i], s1_r.at[1, k - 1, i], zid(k))
            )
        return out_copies

    nq = 16 * NX * NZ
    lanes_q = iota((nq, 128), 1)

    def attend(r):
        pltpu.make_async_copy(cache.at[r], cbuf.at[r], c_sem.at[r]).wait()
        q = qall[r].reshape(nq, lw + 64)
        c = cbuf.at[r]
        sc = dot_nt(q[:, :lw], c[:, :lw]) + dot_nt(q[:, lw:], c[:, lw:])
        place = s * blk + iota((1, blk), 1)
        sc = sc + jnp.where(place < lens[r], 0.0, LOW)
        top = jnp.max(sc, axis=1, keepdims=True)
        w = jnp.exp2((sc - top) * scale2)
        den = jnp.sum(w, axis=1, keepdims=True)
        num = dot(w.astype(BF16), c[:, :lw])
        pout[r] = (num * (1.0 / den)).astype(BF16).reshape(NX, NZ, 16, lw)
        lse = top * scale2 + jnp.log2(den)
        old = stat[...].reshape(nq, 128)
        stat[...] = jnp.where(lanes_q == r, lse, old).reshape(NX, NZ, 16, 128)

    ahead = 3
    for i in range(ahead):
        start(direct(i))
    relay(0)

    def step(i, carry):
        @pl.when(i + ahead < half)
        def _():
            start(direct(i + ahead))

        @pl.when(i + 1 < half)
        def _():
            relay(i + 1)

        for c in onward_in(i):
            c.wait_recv()
        attend(i)
        attend(half + i)
        start(scatter1(i))
        return carry

    lax.fori_loop(0, half, step, 0)

    stats1 = []
    for k in (1, 3, 2):
        stats1.append(rcopy(stat.at[lax.rem(x + k, NX)], st1.at[0, k - 1],
                            t1_s.at[0, k - 1], t1_r.at[0, k - 1], xid(k)))
        stats1.append(rcopy(stat.at[:, lax.rem(z + k, NZ)], st1.at[1, k - 1],
                            t1_s.at[1, k - 1], t1_r.at[1, k - 1], zid(k)))
    start(stats1)
    for c in stats1:
        c.wait_recv()

    def weights(first, others):
        top = functools.reduce(jnp.maximum, others, first)
        ws = [jnp.exp2(v - top) for v in [first] + others]
        total = functools.reduce(jnp.add, ws)
        inv = 1.0 / total
        return [w * inv for w in ws], top + jnp.log2(total)

    def column(w, r):
        return jnp.sum(jnp.where(iota(w.shape, 1) == r, w, 0.0), axis=1, keepdims=True)

    wa, la = weights(stat[x].reshape(64, 128), [st1[0, k].reshape(64, 128) for k in range(3)])
    wb, lb = weights(stat[:, z].reshape(64, 128), [st1[1, k].reshape(64, 128) for k in range(3)])
    stat2[0] = la.reshape(4, 16, 128)
    stat2[1] = lb.reshape(4, 16, 128)
    stats2 = []
    for k in (1, 3, 2):
        stats2.append(rcopy(stat2.at[0, lax.rem(z + k, NZ)], st2.at[0, k - 1],
                            t2_s.at[0, k - 1], t2_r.at[0, k - 1], zid(k)))
        stats2.append(rcopy(stat2.at[1, lax.rem(x + k, NX)], st2.at[1, k - 1],
                            t2_s.at[1, k - 1], t2_r.at[1, k - 1], xid(k)))
    start(stats2)

    def scatter2(i):
        out_copies = []
        for k in (1, 3, 2):
            out_copies.append(
                rcopy(red1.at[0, i, lax.rem(z + k, NZ)], r2.at[0, k - 1, i],
                      s2_s.at[0, k - 1, i], s2_r.at[0, k - 1, i], zid(k))
            )
            out_copies.append(
                rcopy(red1.at[1, i, lax.rem(x + k, NX)], r2.at[1, k - 1, i],
                      s2_s.at[1, k - 1, i], s2_r.at[1, k - 1, i], xid(k))
            )
        return out_copies

    def reduce1(i, carry):
        for c in scatter1(i):
            c.wait_recv()
        acc = column(wa[0], i) * pout[i, x].reshape(64, lw).astype(F32)
        for k in range(3):
            acc += column(wa[k + 1], i) * r1[0, k, i].reshape(64, lw).astype(F32)
        red1[0, i] = acc.astype(BF16).reshape(4, 16, lw)
        acc = column(wb[0], half + i) * pout[half + i, :, z].reshape(64, lw).astype(F32)
        for k in range(3):
            acc += column(wb[k + 1], half + i) * r1[1, k, i].reshape(64, lw).astype(F32)
        red1[1, i] = acc.astype(BF16).reshape(4, 16, lw)
        start(scatter2(i))
        return carry

    lax.fori_loop(0, half, reduce1, 0)

    for c in stats2:
        c.wait_recv()
    va, ma = weights(stat2[0, z], [st2[0, k] for k in range(3)])
    vb, mb = weights(stat2[1, x], [st2[1, k] for k in range(3)])

    def reduce2(i, carry):
        for c in scatter2(i):
            c.wait_recv()
        acc = column(va[0], i) * red1[0, i, z].astype(F32)
        for k in range(3):
            acc += column(va[k + 1], i) * r2[0, k, i].astype(F32)
        fin[i] = acc
        flse[i] = jnp.broadcast_to(column(ma, i), (16, 128))
        acc = column(vb[0], half + i) * red1[1, i, x].astype(F32)
        for k in range(3):
            acc += column(vb[k + 1], half + i) * r2[1, k, i].astype(F32)
        fin[half + i] = acc
        flse[half + i] = jnp.broadcast_to(column(mb, half + i), (16, 128))
        return carry

    lax.fori_loop(0, half, reduce2, 0)

    qo = qall[:, x, z].reshape(rows, lw + 64)
    fresh = dot_nt(qo[:, :lw], latrep[:, :lw]) + dot_nt(qo[:, lw:], latrep[:, lw:])
    ri = iota((rows, rows), 0)
    ci = iota((rows, rows), 1)
    seen = (ri // 16 == ci // 16) & ((ci // 8) % 2 <= (ri // 8) % 2) & (ci % 8 == 0)
    fresh = jnp.where(seen, fresh * scale2, LOW)
    lse = flse[...].reshape(rows, 128)[:, :1]
    top = jnp.maximum(jnp.max(fresh, axis=1, keepdims=True), lse)
    wf = jnp.where(seen, jnp.exp2(fresh - top), 0.0)
    wc = jnp.exp2(lse - top)
    den = wc + jnp.sum(wf, axis=1, keepdims=True)
    num = wc * fin[...].reshape(rows, lw) + dot(wf.astype(BF16), latrep[:, :lw])
    latent = (num * (1.0 / den)).astype(BF16)
    row_b = iota((bl, rows), 0)
    b0 = pick(row_b == sig_row[...])
    b1 = pick(row_b == sig_row[...] + 2 * CAP)
    hrow = iota((rows, 128), 0) % 8
    for j in range(4):
        va0 = jnp.where(hrow == j, dot(latent, w_v[j]), 0.0).astype(BF16)
        vb0 = jnp.where(hrow == j + 4, dot(latent, w_v[j + 4]), 0.0).astype(BF16)
        back = dot(b0, va0) + dot(b1, vb0)
        tx2[:, :, j * 128 : (j + 1) * 128] = back.astype(BF16).reshape(ngrp, 16, 128)

    home = [
        rcopy(tx2.at[lax.rem(g + k, ngrp)], rx2.at[g], rb_s.at[k], rb_r.at[k], gid(k))
        for k in range(1, ngrp)
    ]
    start(home)
    rx2[g] = tx2[g]
    for k in range(1, ngrp):
        src = lax.rem(g + ngrp - k, ngrp)
        rcopy(tx2.at[src], rx2.at[src], rb_s.at[k], rb_r.at[k], gid(k)).wait_recv()
    col_b = iota((2 * nreq, bl), 1)
    got = rx2[...].reshape(bl, lw)
    out[:, :lw] = dot(pick(col_b == rho_col[...]), got).astype(BF16)
    out[:, lw:] = dot(pick(col_b == rho_col[...] + 2 * CAP), got).astype(BF16)

    for c in route + gather1 + stats1 + stats2 + home:
        c.wait_send()

    def drain(i, carry):
        for c in direct(i) + onward(i) + scatter1(i) + scatter2(i):
            c.wait_send()
        return carry

    lax.fori_loop(0, half, drain, 0)


def on_device(
    prefill_cache, lengths, decode_slots, q_nope, q_pe, new_latent, w_uk, value_up_weight
):
    ngrp = lax.axis_size("grp")
    me = lax.axis_index("grp")
    nreq, blk, width = prefill_cache.shape
    steps = new_latent.shape[0]
    heads, nope, lw = w_uk.shape
    half = nreq // 2
    scale2 = (nope + width - lw) ** -0.5 * LOG2E

    dest = decode_slots // nreq
    places = jnp.arange(nreq, dtype=jnp.int32)
    same = (dest[:, :, None] == dest[:, None, :]) & (places[None, :] < places[:, None])[None]
    code = 2 * jnp.sum(same.astype(jnp.int32), axis=2)
    my_slots = lax.dynamic_index_in_dim(decode_slots, me, 0, keepdims=False)
    my_code = lax.dynamic_index_in_dim(code, me, 0, keepdims=False)
    ticks = jnp.arange(steps, dtype=jnp.int32)
    rho = (ticks[:, None] + (my_slots // nreq * 16 + my_code)[None, :]).reshape(-1)
    origin = (jnp.arange(ngrp, dtype=jnp.int32)[:, None] * 16 + code).reshape(-1)
    match = decode_slots.reshape(-1)[None, :] == (me * nreq + places)[:, None]
    sig = jnp.sum(jnp.where(match, origin[None, :], 0), axis=1)
    sig = jnp.broadcast_to(
        sig[:, None, None] + ticks[None, :, None], (nreq, steps, heads)
    ).reshape(-1)
    lens = lax.dynamic_slice_in_dim(lengths, me * nreq, nreq, 0)

    rows = nreq * steps * heads
    vm = pl.BlockSpec(memory_space=pltpu.VMEM)
    dma = pltpu.SemaphoreType.DMA
    bytes_in = 2 * prefill_cache.size
    out = pl.pallas_call(
        functools.partial(kernel, ngrp, nreq, blk, scale2),
        out_shape=jax.ShapeDtypeStruct((steps * nreq, heads * 128), BF16),
        in_specs=[pl.BlockSpec(memory_space=pltpu.SMEM)] + [vm] * 9
        + [pl.BlockSpec(memory_space=pl.ANY)],
        out_specs=vm,
        scratch_shapes=[
            pltpu.VMEM((nreq, blk, width), BF16),
            pltpu.VMEM((ngrp, 16, 1088), BF16),
            pltpu.VMEM((ngrp, 16, 1088), BF16),
            pltpu.VMEM((rows, width), BF16),
            pltpu.VMEM((nreq, NX, NZ, 16, width), BF16),
            pltpu.VMEM((nreq, NX, NZ, 16, lw), BF16),
            pltpu.VMEM((NX, NZ, 16, 128), F32),
            pltpu.VMEM((2, 3, half, 4, 16, lw), BF16),
            pltpu.VMEM((2, 3, 4, 16, 128), F32),
            pltpu.VMEM((2, half, 4, 16, lw), BF16),
            pltpu.VMEM((2, 4, 16, 128), F32),
            pltpu.VMEM((2, 3, half, 16, lw), BF16),
            pltpu.VMEM((2, 3, 16, 128), F32),
            pltpu.VMEM((nreq, 16, lw), F32),
            pltpu.VMEM((nreq, 16, 128), F32),
            pltpu.VMEM((ngrp, 16, lw), BF16),
            pltpu.VMEM((ngrp, 16, lw), BF16),
            dma((nreq,)),
            dma((ngrp,)), dma((ngrp,)),
            dma((2, 4)), dma((2, 4)),
            dma((2, 4, half)), dma((2, 4, half)),
            dma((2, 3, half)), dma((2, 3, half)),
            dma((2, 3)), dma((2, 3)),
            dma((2, 3, half)), dma((2, 3, half)),
            dma((2, 3)), dma((2, 3)),
            dma((ngrp,)), dma((ngrp,)),
        ],
        compiler_params=pltpu.CompilerParams(
            collective_id=0, has_side_effects=True, vmem_limit_bytes=58 * 1024 * 1024
        ),
        cost_estimate=pl.CostEstimate(
            flops=2 * nreq * 256 * blk * (width + lw), bytes_accessed=bytes_in,
            transcendentals=nreq * 256 * blk,
        ),
    )(
        lens, rho[None, :], rho[:, None], sig[None, :], sig[:, None],
        q_nope.reshape(steps * nreq, -1), q_pe.reshape(steps * nreq, -1),
        new_latent.reshape(steps * nreq, -1), w_uk.reshape(heads * nope, lw),
        value_up_weight, prefill_cache,
    )
    return out.reshape(steps, nreq, -1)


def solution(mesh):
    return jax.shard_map(
        on_device,
        mesh=mesh,
        in_specs=(
            P("grp", "seq", None),
            P(),
            P(),
            P(None, "grp", "seq"),
            P(None, "grp", "seq"),
            P(None, "grp", None),
            P("seq", None, None),
            P("seq", None, None),
        ),
        out_specs=P(None, "grp", "seq"),
        check_vma=False,
    )
```

```python
import functools

import jax
import jax.numpy as jnp
from jax import lax
from jax.experimental import pallas as pl
from jax.experimental.pallas import tpu as pltpu
from jax.sharding import PartitionSpec as P

MESH = pl.DeviceIdType.MESH
LOG2E = 1.4426950408889634
LOW = -1e30
CAP = 3
NX = 4
NZ = 4
F32 = jnp.float32
BF16 = jnp.bfloat16


def dot(a, b):
    return jnp.dot(a, b, preferred_element_type=F32)


def dot_nt(a, b):
    return lax.dot_general(a, b, (((1,), (1,)), ((), ())), preferred_element_type=F32)


def iota(shape, dim):
    return lax.broadcasted_iota(jnp.int32, shape, dim)


def pick(cond):
    return jnp.where(cond, 1.0, 0.0).astype(BF16)


def kernel(
    ngrp, nreq, blk, scale2,
    lens, slots, qn, qp, lat, w_uk_hbm, w_v_hbm, cache,
    out,
    cbuf, w_uk, w_v, tx, rx, latrep, qall, pout, lrow, h1, lh1, r1, lr1, red1, lred, r2, lr2,
    fin, flse, tx2, rx2,
    c_sem, w_sem, out_sem, rt_r, rb_r, g1_r, g2_r, g3_r, h_r, s1_r, s2_r,
):
    g = lax.axis_index("grp")
    s = lax.axis_index("seq")
    x = lax.div(s, NZ)
    z = lax.rem(s, NZ)
    half = nreq // 2
    rows = nreq * 16
    lw = 512
    c_copies = [pltpu.make_async_copy(cache.at[r], cbuf.at[r], c_sem.at[r]) for r in range(nreq)]
    w_copies = [
        pltpu.make_async_copy(w_uk_hbm, w_uk, w_sem.at[0]),
        pltpu.make_async_copy(w_v_hbm, w_v, w_sem.at[1]),
    ]
    for c in w_copies + c_copies:
        c.start()

    def gid(k):
        return {"grp": lax.rem(g + k, ngrp)}

    def xid(k):
        return {"seq": lax.rem(x + k, NX) * NZ + z}

    def zid(k):
        return {"seq": x * NZ + lax.rem(z + k, NZ)}

    def rcopy(src, dst, ss, rs, dev):
        return pltpu.make_async_remote_copy(
            src_ref=src, dst_ref=dst, send_sem=ss, recv_sem=rs, device_id=dev, device_id_type=MESH
        )

    barrier = pltpu.get_barrier_semaphore()
    for k in range(1, ngrp):
        pl.semaphore_signal(barrier, inc=1, device_id=gid(k), device_id_type=MESH)
    for k in range(1, 4):
        pl.semaphore_signal(barrier, inc=1, device_id=xid(k), device_id_type=MESH)
        pl.semaphore_signal(barrier, inc=1, device_id=zid(k), device_id_type=MESH)

    shift = nreq.bit_length() - 1
    served = slots[...]
    dest = lax.shift_right_logical(served, shift)
    lane_s = iota((ngrp, nreq), 1)
    rank = jnp.zeros((ngrp, nreq), jnp.int32)
    for j in range(nreq - 1):
        rank += jnp.where((dest == dest[:, j : j + 1]) & (lane_s > j), 1, 0)
    origin = iota((ngrp, nreq), 0) * 16 + 2 * rank
    mine = iota((ngrp, nreq), 0) == g
    rho = jnp.sum(jnp.where(mine, dest * 16 + 2 * rank, 0), axis=0, keepdims=True)
    row_id = iota((rows, nreq), 0)
    asked = g * nreq + row_id // 16
    sig = jnp.zeros((rows, nreq), jnp.int32)
    for j in range(ngrp):
        sig += jnp.where(served[j : j + 1, :] == asked, origin[j : j + 1, :], 0)
    sig = jnp.sum(sig, axis=1, keepdims=True) + (iota((rows, 1), 0) // 8) % 2

    bl = ngrp * 16
    row_l = iota((bl, nreq), 0)
    sends = [[jnp.where(row_l == rho + t + 2 * CAP * f, 1.0, 0.0) for t in range(2)] for f in range(2)]

    def send_dot(f, cols):
        both = [dot(sends[f][t].astype(BF16), cols(pl.ds(t * nreq, nreq))) for t in range(2)]
        return both[0] + both[1]

    head = send_dot(0, lambda r: qn[r, :lw]) + send_dot(1, lambda r: qp[r, :])
    tx[:, :, :lw] = head.astype(BF16).reshape(ngrp, 16, lw)
    mid = send_dot(0, lambda r: qn[r, lw:]) + send_dot(1, lambda r: lat[r, :lw])
    tx[:, :, lw : 2 * lw] = mid.astype(BF16).reshape(ngrp, 16, lw)
    tail = send_dot(1, lambda r: lat[r, lw:])
    tx[:, :, 2 * lw :] = tail.astype(BF16).reshape(ngrp, 16, 64)

    pl.semaphore_wait(barrier, ngrp - 1 + 6)
    route = [
        rcopy(tx.at[lax.rem(g + k, ngrp)], rx.at[g], out_sem.at[9], rt_r.at[0], gid(k))
        for k in range(1, ngrp)
    ]
    for c in route:
        c.start()
    rx[g] = tx[g]
    most = pl.ds(0, ngrp - 1)
    all_routed = rcopy(tx.at[most], rx.at[most], out_sem.at[9], rt_r.at[0], gid(1))
    all_routed.wait_recv()

    col_l = iota((rows, bl), 1)
    pulls = [jnp.where(col_l == sig + 2 * CAP * f, 1.0, 0.0) for f in range(2)]
    m0, m1 = [v.astype(BF16) for v in pulls]
    own = iota((rows, lw), 0) % 8
    lane = iota((rows, lw), 1)
    w_copies[0].wait()
    absorbed = jnp.zeros((rows, lw), F32)
    for j in range(2):
        spread = dot(m0, rx[:, :, j * lw : (j + 1) * lw].reshape(bl, lw))
        spread = jnp.where(lane // 128 + 4 * j == own, spread, 0.0).astype(BF16)
        absorbed += dot(spread, w_uk[j * lw : (j + 1) * lw, :])
    qall[:, x, z, :, :lw] = absorbed.astype(BF16).reshape(nreq, 16, lw)
    spread = dot(m1, rx[:, :, :lw].reshape(bl, lw))
    spread = jnp.where(lane // 64 == own, spread, 0.0).astype(BF16)
    fold = pick(iota((lw, 64), 0) % 64 == iota((lw, 64), 1))
    qall[:, x, z, :, lw:] = dot(spread, fold).astype(BF16).reshape(nreq, 16, 64)

    xl = lax.rem(x + 3, NX)
    xr = lax.rem(x + 1, NX)
    xo = lax.rem(x + 2, NX)
    zl = lax.rem(z + 3, NZ)
    zr = lax.rem(z + 1, NZ)
    zo = lax.rem(z + 2, NZ)
    two = (pl.ds(0, 2), pl.ds(2, 2))

    def start(copies):
        for c in copies:
            c.start()

    def landed(ref, sem):
        rcopy(ref, ref, out_sem.at[0], sem, xid(1)).wait_recv()

    def near(i):
        copies = []
        for k in (1, 3, 2):
            a, b = qall.at[i, x, z], qall.at[half + i, x, z]
            copies.append(rcopy(a, a, out_sem.at[0], g1_r.at[i], zid(k)))
            copies.append(rcopy(b, b, out_sem.at[0], g1_r.at[i], xid(k)))
        return copies

    def near_in(i):
        landed(qall.at[i, pl.ds(0, 2), pl.ds(0, 3)], g1_r.at[i])

    def direct(i):
        a = qall.at[i, x]
        b = qall.at[half + i, :, z]
        return [
            rcopy(ref, ref, out_sem.at[1], g2_r.at[i], dev)
            for ref, dev in ((a, xid(1)), (b, zid(1)), (a, xid(3)), (b, zid(3)))
        ]

    def direct_in(i):
        landed(qall.at[i], g2_r.at[i])

    def onward(i):
        moves = (
            (qall.at[i, xl, two[0]], xid(1)), (qall.at[half + i, two[0], zl], zid(1)),
            (qall.at[i, xr, two[1]], xid(3)), (qall.at[half + i, two[1], zr], zid(3)),
        )
        return [rcopy(ref, ref, out_sem.at[2], g3_r.at[i], dev) for ref, dev in moves]

    def onward_in(i):
        landed(qall.at[i, pl.ds(0, 2)], g3_r.at[i])

    def relay(i):
        direct_in(i)
        start(onward(i))

    first = 2
    for i in range(first):
        start(near(i))

    latrep[:, :lw] = dot(m1, rx[:, :, lw : 2 * lw].reshape(bl, lw)).astype(BF16)
    latrep[:, lw:] = dot(m1, rx[:, :, 2 * lw :].reshape(bl, 64)).astype(BF16)
    qo = qall[:, x, z].reshape(rows, lw + 64)
    fresh = dot_nt(qo[:, :lw], latrep[:, :lw]) + dot_nt(qo[:, lw:], latrep[:, lw:])
    ri = iota((rows, rows), 0)
    ci = iota((rows, rows), 1)
    seen = (ri // 16 == ci // 16) & ((ci // 8) % 2 <= (ri // 8) % 2) & (ci % 8 == 0)
    fresh = jnp.where(seen, fresh * scale2, LOW)
    ftop = jnp.max(fresh, axis=1, keepdims=True)
    wf = jnp.where(seen, jnp.exp2(fresh - ftop), 0.0)
    fden = jnp.sum(wf, axis=1, keepdims=True)
    fnum = dot(wf.astype(BF16), latrep[:, :lw])

    def send(src, dst, ls, ld, n, rs, i, dev):
        return [
            rcopy(src, dst, out_sem.at[n], rs.at[0, i], dev),
            rcopy(ls, ld, out_sem.at[n + 1], rs.at[1, i], dev),
        ]

    def far(i):
        copies = []
        for j in range(2):
            a, b = pout.at[i, xo, two[j]], pout.at[half + i, two[j], zo]
            copies += send(a, h1.at[0, j, i], lrow.at[i, xo], lh1.at[0, j, i], 3, h_r, i,
                           xid(1 + 2 * j))
            copies += send(b, h1.at[1, j, i], lrow.at[half + i, zo], lh1.at[1, j, i], 3, h_r, i,
                           zid(1 + 2 * j))
        return copies

    def far_in(i):
        landed(pout.at[i, pl.ds(0, 2)], h_r.at[0, i])
        landed(lrow.at[i], h_r.at[1, i])

    def scatter1(i):
        copies = []
        for j in range(2):
            xt, zt = (xr, xl)[j], (zr, zl)[j]
            copies += send(pout.at[i, xt], r1.at[0, j, i], lrow.at[i, xt], lr1.at[0, j, i],
                           5, s1_r, i, xid(1 + 2 * j))
            copies += send(pout.at[half + i, :, zt], r1.at[1, j, i], lrow.at[half + i, zt],
                           lr1.at[1, j, i], 5, s1_r, i, zid(1 + 2 * j))
        return copies

    def scatter1_in(i):
        landed(pout.at[i], s1_r.at[0, i])
        landed(lrow.at[i], s1_r.at[1, i])

    def scatter2(i):
        copies = []
        for k in (1, 3, 2):
            copies += send(red1.at[0, i, lax.rem(z + k, NZ)], r2.at[0, k - 1, i], lred.at[0, i],
                           lr2.at[0, k - 1, i], 7, s2_r, i, zid(k))
            copies += send(red1.at[1, i, lax.rem(x + k, NX)], r2.at[1, k - 1, i], lred.at[1, i],
                           lr2.at[1, k - 1, i], 7, s2_r, i, xid(k))
        return copies

    def scatter2_in(i):
        landed(pout.at[i, pl.ds(0, 2), pl.ds(0, 3)], s2_r.at[0, i])
        landed(lrow.at[pl.ds(0, 2), pl.ds(0, 3)], s2_r.at[1, i])

    def weights(ls):
        top = functools.reduce(jnp.maximum, ls)
        ws = [jnp.exp2(v - top) for v in ls]
        total = functools.reduce(jnp.add, ws)
        inv = 1.0 / total
        return [w * inv for w in ws], top + jnp.log2(total)

    def column(w, n, off):
        shape = (n, 128)
        return jnp.sum(
            jnp.where(iota(shape, 1) == iota(shape, 0) + off, w, 0.0), axis=1, keepdims=True
        )

    def blend(blocks, ws, n, off):
        acc = 0.0
        for b, w in zip(blocks, ws):
            acc += column(w, n, off) * b.reshape(n, lw).astype(F32)
        return acc

    nq = 16 * NX * NZ
    row_q = iota((nq, 128), 0)
    lane_q = iota((nq, 128), 1)

    def attend(r, part):
        pltpu.make_async_copy(cache.at[r], cbuf.at[r], c_sem.at[r]).wait()
        q = qall[r].reshape(nq, lw + 64)
        c = cbuf.at[r]
        sc = dot(q[:, :lw], c[:lw, :]) + dot(q[:, lw:], c[lw:, :])
        place = s * blk + iota((1, blk), 1)
        sc = sc + jnp.where(place < lens[g * nreq + r], 0.0, LOW)
        top = jnp.max(sc, axis=1, keepdims=True)
        w = jnp.exp2((sc - top) * scale2)
        den = jnp.sum(w, axis=1, keepdims=True)
        num = dot_nt(w.astype(BF16), c[:lw, :])
        pout[r] = (num * (1.0 / den)).astype(BF16).reshape(NX, NZ, 16, lw)
        lse = top * scale2 + jnp.log2(den)
        if part == 0:
            diag = jnp.where(lane_q == row_q % 64, lse, 0.0).reshape(4, 64, 128)
        else:
            diag = jnp.where(lane_q == row_q // 64 * 16 + row_q % 16, lse, 0.0)
            diag = jnp.sum(diag.reshape(4, 4, 16, 128), axis=0)
        for d in range(4):
            lrow[r, d] = jnp.sum(diag[d], axis=0, keepdims=True)

    lane_1 = iota((1, 128), 1)

    def middle(i):
        for j in range(2):
            xt, zt = (xr, xl)[j], (zr, zl)[j]
            keep = (lane_1 < 32) if j == 0 else (lane_1 >= 32)
            ws, ln = weights([lrow[i, xt], lh1[0, j, i]])
            acc = blend([pout[i, xt, two[j]], h1[0, j, i]], ws, 32, 32 * j)
            pout[i, xt, two[j]] = acc.astype(BF16).reshape(2, 16, lw)
            lrow[i, xt] = jnp.where(keep, ln, lrow[i, xt])
            r = half + i
            ws, ln = weights([lrow[r, zt], lh1[1, j, i]])
            acc = blend([pout[r, two[j], zt], h1[1, j, i]], ws, 32, 32 * j)
            pout[r, two[j], zt] = acc.astype(BF16).reshape(2, 16, lw)
            lrow[r, zt] = jnp.where(keep, ln, lrow[r, zt])

    def reduce1(i):
        ws, ln = weights([lrow[i, x], lr1[0, 0, i], lr1[0, 1, i]])
        acc = blend([pout[i, x], r1[0, 0, i], r1[0, 1, i]], ws, 64, 0)
        red1[0, i] = acc.astype(BF16).reshape(4, 16, lw)
        lred[0, i] = ln
        ws, ln = weights([lrow[half + i, z], lr1[1, 0, i], lr1[1, 1, i]])
        acc = blend([pout[half + i, :, z], r1[1, 0, i], r1[1, 1, i]], ws, 64, 0)
        red1[1, i] = acc.astype(BF16).reshape(4, 16, lw)
        lred[1, i] = ln

    def reduce2(i):
        for part, own in ((0, z), (1, x)):
            ws, ln = weights([lred[part, i]] + [lr2[part, k, i] for k in range(3)])
            blocks = [red1[part, i, own]] + [r2[part, k, i] for k in range(3)]
            fin[part * half + i] = blend(blocks, ws, 16, own * 16)
            flse[part * half + i] = jnp.broadcast_to(column(ln, 16, own * 16), (16, 128))

    def step(t, carry):
        @pl.when(t + first < half)
        def _():
            start(near(t + first))

        @pl.when(t < half)
        def _():
            near_in(t)
            start(direct(t))

        i1 = t - 1

        @pl.when((i1 >= 0) & (i1 < half))
        def _():
            relay(i1)

        i2 = t - 2

        @pl.when((i2 >= 0) & (i2 < half))
        def _():
            onward_in(i2)
            attend(i2, 0)
            attend(half + i2, 1)
            start(far(i2))

        i3 = t - 3

        @pl.when((i3 >= 0) & (i3 < half))
        def _():
            far_in(i3)
            middle(i3)
            start(scatter1(i3))

        i5 = t - 5

        @pl.when((i5 >= 0) & (i5 < half))
        def _():
            scatter1_in(i5)
            reduce1(i5)
            start(scatter2(i5))

        i7 = t - 7

        @pl.when(i7 >= 0)
        def _():
            scatter2_in(i7)
            reduce2(i7)

        return carry

    lax.fori_loop(0, half + 7, step, 0)

    w_copies[1].wait()
    lse = flse[...].reshape(rows, 128)[:, :1]
    top = jnp.maximum(ftop, lse)
    wc = jnp.exp2(lse - top)
    wn = jnp.exp2(ftop - top)
    den = wc + wn * fden
    num = wc * fin[...].reshape(rows, lw) + wn * fnum
    latent = (num * (1.0 / den)).astype(BF16)
    b0, b1 = [v.T.astype(BF16) for v in pulls]
    hrow = iota((rows, 128), 0) % 8
    for j in range(4):
        va0 = jnp.where(hrow == j, dot(latent, w_v[j]), 0.0).astype(BF16)
        vb0 = jnp.where(hrow == j + 4, dot(latent, w_v[j + 4]), 0.0).astype(BF16)
        back = dot(b0, va0) + dot(b1, vb0)
        tx2[:, :, j * 128 : (j + 1) * 128] = back.astype(BF16).reshape(ngrp, 16, 128)

    home = [
        rcopy(tx2.at[lax.rem(g + k, ngrp)], rx2.at[g], out_sem.at[10], rb_r.at[0], gid(k))
        for k in range(1, ngrp)
    ]
    start(home)
    rx2[g] = tx2[g]

    def left(ref, n):
        rcopy(ref, ref, out_sem.at[n], s1_r.at[0, 0], xid(1)).wait_send()

    left(qall.at[pl.ds(0, 3)], 0)
    left(qall.at[pl.ds(0, 8)], 1)
    left(qall.at[pl.ds(0, 4)], 2)
    left(pout.at[pl.ds(0, 4)], 3)
    left(lrow.at[pl.ds(0, 8)], 4)
    left(pout.at[pl.ds(0, 8)], 5)
    left(lrow.at[pl.ds(0, 8)], 6)
    left(pout.at[pl.ds(0, 3)], 7)
    left(lrow.at[pl.ds(0, 12)], 8)
    all_routed.wait_send()
    all_home = rcopy(tx2.at[most], rx2.at[most], out_sem.at[10], rb_r.at[0], gid(1))
    all_home.wait_recv()
    got = rx2[...].reshape(bl, lw)
    for f in range(2):
        for t in range(2):
            kept = dot(sends[f][t].T.astype(BF16), got)
            out[pl.ds(t * nreq, nreq), pl.ds(f * lw, lw)] = kept.astype(BF16)

    all_home.wait_send()


def on_device(
    prefill_cache, lengths, decode_slots, q_nope, q_pe, new_latent, w_uk, value_up_weight
):
    ngrp = lax.axis_size("grp")
    nreq, blk, width = prefill_cache.shape
    steps = new_latent.shape[0]
    heads, nope, lw = w_uk.shape
    half = nreq // 2
    scale2 = (nope + width - lw) ** -0.5 * LOG2E

    rows = nreq * steps * heads
    vm = pl.BlockSpec(memory_space=pltpu.VMEM)
    dma = pltpu.SemaphoreType.DMA
    bytes_in = 2 * prefill_cache.size
    out = pl.pallas_call(
        functools.partial(kernel, ngrp, nreq, blk, scale2),
        out_shape=jax.ShapeDtypeStruct((steps * nreq, heads * 128), BF16),
        in_specs=[pl.BlockSpec(memory_space=pltpu.SMEM)] + [vm] * 4
        + [pl.BlockSpec(memory_space=pl.ANY)] * 3,
        out_specs=vm,
        scratch_shapes=[
            pltpu.VMEM((nreq, width, blk), BF16),
            pltpu.VMEM((heads * nope, lw), BF16),
            pltpu.VMEM((heads, lw, 128), BF16),
            pltpu.VMEM((ngrp, 16, 1088), BF16),
            pltpu.VMEM((ngrp, 16, 1088), BF16),
            pltpu.VMEM((rows, width), BF16),
            pltpu.VMEM((nreq, NX, NZ, 16, width), BF16),
            pltpu.VMEM((nreq, NX, NZ, 16, lw), BF16),
            pltpu.VMEM((nreq, 4, 1, 128), F32),
            pltpu.VMEM((2, 2, half, 2, 16, lw), BF16),
            pltpu.VMEM((2, 2, half, 1, 128), F32),
            pltpu.VMEM((2, 2, half, 4, 16, lw), BF16),
            pltpu.VMEM((2, 2, half, 1, 128), F32),
            pltpu.VMEM((2, half, 4, 16, lw), BF16),
            pltpu.VMEM((2, half, 1, 128), F32),
            pltpu.VMEM((2, 3, half, 16, lw), BF16),
            pltpu.VMEM((2, 3, half, 1, 128), F32),
            pltpu.VMEM((nreq, 16, lw), F32),
            pltpu.VMEM((nreq, 16, 128), F32),
            pltpu.VMEM((ngrp, 16, lw), BF16),
            pltpu.VMEM((ngrp, 16, lw), BF16),
            dma((nreq,)), dma((2,)), dma((11,)), dma((1,)), dma((1,)),
            dma((half,)), dma((half,)), dma((half,)),
            dma((2, half)), dma((2, half)), dma((2, half)),
        ],
        compiler_params=pltpu.CompilerParams(
            collective_id=0, has_side_effects=True, vmem_limit_bytes=58 * 1024 * 1024
        ),
        cost_estimate=pl.CostEstimate(
            flops=2 * nreq * 256 * blk * (width + lw), bytes_accessed=bytes_in,
            transcendentals=nreq * 256 * blk,
        ),
    )(
        lengths, decode_slots,
        q_nope.reshape(steps * nreq, -1), q_pe.reshape(steps * nreq, -1),
        new_latent.reshape(steps * nreq, -1), w_uk.reshape(heads * nope, lw),
        value_up_weight, jnp.swapaxes(prefill_cache, 1, 2),
    )
    return out.reshape(steps, nreq, -1)


def solution(mesh):
    return jax.shard_map(
        on_device,
        mesh=mesh,
        in_specs=(
            P("grp", "seq", None),
            P(),
            P(),
            P(None, "grp", "seq"),
            P(None, "grp", "seq"),
            P(None, "grp", None),
            P("seq", None, None),
            P("seq", None, None),
        ),
        out_specs=P(None, "grp", "seq"),
        check_vma=False,
    )
```

```python
import functools

import jax
import jax.numpy as jnp
from jax import lax
from jax.experimental import pallas as pl
from jax.experimental.pallas import tpu as pltpu
from jax.sharding import PartitionSpec as P

MESH = pl.DeviceIdType.MESH
LOG2E = 1.4426950408889634
LOW = -1e30
CAP = 3
NX = 4
NZ = 4
F32 = jnp.float32
BF16 = jnp.bfloat16


def dot(a, b):
    return jnp.dot(a, b, preferred_element_type=F32)


def dot_nt(a, b):
    return lax.dot_general(a, b, (((1,), (1,)), ((), ())), preferred_element_type=F32)


def iota(shape, dim):
    return lax.broadcasted_iota(jnp.int32, shape, dim)


def pick(cond):
    return jnp.where(cond, 1.0, 0.0).astype(BF16)


def kernel(
    ngrp, nreq, blk, scale2,
    lens, slots, qn, qp, lat, w_uk_hbm, w_v_hbm, cache,
    out,
    cbuf, w_uk, w_v, tx, rx, ty, ry, latrep, qall, qpe, pout, lrow, h1, lh1, r1, lr1, rd, lrd, red1, lred, r2, lr2,
    fin, flse, tx2, rx2,
    c_sem, w_sem, out_sem, rt_r, ru_r, rb_r, g1_r, g2_r, g3_r, e1_r, e2_r, e3_r, h_r, s1_r, s2_r,
):
    g = lax.axis_index("grp")
    s = lax.axis_index("seq")
    x = lax.div(s, NZ)
    z = lax.rem(s, NZ)
    half = nreq // 2
    rows = nreq * 16
    lw = 512
    c_copies = [pltpu.make_async_copy(cache.at[r], cbuf.at[r], c_sem.at[r]) for r in range(nreq)]
    w_copies = [
        pltpu.make_async_copy(w_uk_hbm, w_uk, w_sem.at[0]),
        pltpu.make_async_copy(w_v_hbm, w_v, w_sem.at[1]),
    ]
    for c in w_copies + c_copies:
        c.start()

    def gid(k):
        return {"grp": lax.rem(g + k, ngrp)}

    def xid(k):
        return {"seq": lax.rem(x + k, NX) * NZ + z}

    def zid(k):
        return {"seq": x * NZ + lax.rem(z + k, NZ)}

    def rcopy(src, dst, ss, rs, dev):
        return pltpu.make_async_remote_copy(
            src_ref=src, dst_ref=dst, send_sem=ss, recv_sem=rs, device_id=dev, device_id_type=MESH
        )

    barrier = pltpu.get_barrier_semaphore()
    for k in range(1, ngrp):
        pl.semaphore_signal(barrier, inc=1, device_id=gid(k), device_id_type=MESH)
    for k in range(1, 4):
        pl.semaphore_signal(barrier, inc=1, device_id=xid(k), device_id_type=MESH)
        pl.semaphore_signal(barrier, inc=1, device_id=zid(k), device_id_type=MESH)

    shift = nreq.bit_length() - 1
    served = slots[...]
    dest = lax.shift_right_logical(served, shift)
    lane_s = iota((ngrp, nreq), 1)
    rank = jnp.zeros((ngrp, nreq), jnp.int32)
    for j in range(nreq - 1):
        rank += jnp.where((dest == dest[:, j : j + 1]) & (lane_s > j), 1, 0)
    origin = iota((ngrp, nreq), 0) * 16 + 2 * rank
    mine = iota((ngrp, nreq), 0) == g
    rho = jnp.sum(jnp.where(mine, dest * 16 + 2 * rank, 0), axis=0, keepdims=True)
    row_id = iota((rows, nreq), 0)
    asked = g * nreq + row_id // 16
    sig = jnp.zeros((rows, nreq), jnp.int32)
    for j in range(ngrp):
        sig += jnp.where(served[j : j + 1, :] == asked, origin[j : j + 1, :], 0)
    sig = jnp.sum(sig, axis=1, keepdims=True) + (iota((rows, 1), 0) // 8) % 2

    bl = ngrp * 16
    row_l = iota((bl, nreq), 0)
    sends = [[jnp.where(row_l == rho + t + 2 * CAP * f, 1.0, 0.0) for t in range(2)] for f in range(2)]

    def send_dot(f, cols):
        both = [dot(sends[f][t].astype(BF16), cols(pl.ds(t * nreq, nreq))) for t in range(2)]
        return both[0] + both[1]

    head = send_dot(0, lambda r: qn[r, :lw]) + send_dot(1, lambda r: qn[r, lw:])
    tx[...] = head.astype(BF16).reshape(ngrp, 16, lw)
    mid = send_dot(0, lambda r: qp[r, :]) + send_dot(1, lambda r: lat[r, :lw])
    ty[:, :, :lw] = mid.astype(BF16).reshape(ngrp, 16, lw)
    tail = send_dot(1, lambda r: lat[r, lw:])
    ty[:, :, lw:] = tail.astype(BF16).reshape(ngrp, 16, 64)
    pl.semaphore_wait(barrier, ngrp - 1 + 6)
    dst = [lax.rem(g + k, ngrp) for k in range(1, ngrp)]
    route = [
        rcopy(tx.at[d], rx.at[g], out_sem.at[9], rt_r.at[0], {"grp": d}) for d in dst
    ] + [
        rcopy(ty.at[d], ry.at[g], out_sem.at[14], ru_r.at[0], {"grp": d}) for d in dst
    ]
    for c in route:
        c.start()
    rx[g] = tx[g]
    ry[g] = ty[g]
    most = pl.ds(0, ngrp - 1)
    all_routed = rcopy(tx.at[most], rx.at[most], out_sem.at[9], rt_r.at[0], gid(1))
    more_routed = rcopy(ty.at[most], ry.at[most], out_sem.at[14], ru_r.at[0], gid(1))
    all_routed.wait_recv()

    col_l = iota((rows, bl), 1)
    pulls = [jnp.where(col_l == sig + 2 * CAP * f, 1.0, 0.0) for f in range(2)]
    m0, m1 = [v.astype(BF16) for v in pulls]
    own = iota((rows, lw), 0) % 8
    lane = iota((rows, lw), 1)
    w_copies[0].wait()
    absorbed = jnp.zeros((rows, lw), F32)
    for j in range(2):
        spread = dot((m0, m1)[j], rx[...].reshape(bl, lw))
        spread = jnp.where(lane // 128 + 4 * j == own, spread, 0.0).astype(BF16)
        absorbed += dot(spread, w_uk[j * lw : (j + 1) * lw, :])
    qall[:, x, z] = absorbed.astype(BF16).reshape(nreq, 16, lw)
    xl = lax.rem(x + 3, NX)
    xr = lax.rem(x + 1, NX)
    xo = lax.rem(x + 2, NX)
    zl = lax.rem(z + 3, NZ)
    zr = lax.rem(z + 1, NZ)
    zo = lax.rem(z + 2, NZ)
    two = (pl.ds(0, 2), pl.ds(2, 2))

    def start(copies):
        for c in copies:
            c.start()

    def landed(ref, sem):
        rcopy(ref, ref, out_sem.at[0], sem, xid(1)).wait_recv()

    def near(i):
        copies = []
        for k in (1, 3, 2):
            a, b = qall.at[i, x, z], qall.at[half + i, x, z]
            copies.append(rcopy(a, a, out_sem.at[0], g1_r.at[i], zid(k)))
            copies.append(rcopy(b, b, out_sem.at[0], g1_r.at[i], xid(k)))
        return copies

    def near_in(i):
        landed(qall.at[i, pl.ds(0, 2), pl.ds(0, 3)], g1_r.at[i])

    def direct(i):
        a = qall.at[i, x]
        b = qall.at[half + i, :, z]
        return [
            rcopy(ref, ref, out_sem.at[1], g2_r.at[i], dev)
            for ref, dev in ((a, xid(1)), (b, zid(1)), (a, xid(3)), (b, zid(3)))
        ]

    def direct_in(i):
        landed(qall.at[i], g2_r.at[i])

    def onward(i):
        moves = (
            (qall.at[i, xl, two[0]], xid(1)), (qall.at[half + i, two[0], zl], zid(1)),
            (qall.at[i, xr, two[1]], xid(3)), (qall.at[half + i, two[1], zr], zid(3)),
        )
        return [rcopy(ref, ref, out_sem.at[2], g3_r.at[i], dev) for ref, dev in moves]

    def onward_in(i):
        landed(qall.at[i, pl.ds(0, 2)], g3_r.at[i])

    def relay(i):
        direct_in(i)
        start(onward(i))

    quarter = half // 2

    def near_pe(i):
        copies = []
        for k in (1, 3, 2):
            a, b = qpe.at[i, x, z], qpe.at[quarter + i, x, z]
            copies.append(rcopy(a, a, out_sem.at[11], e1_r.at[i], zid(k)))
            copies.append(rcopy(b, b, out_sem.at[11], e1_r.at[i], xid(k)))
        return copies

    def near_pe_in(i):
        landed(qpe.at[i, pl.ds(0, 2), pl.ds(0, 3)], e1_r.at[i])

    def direct_pe(i):
        a = qpe.at[i, x]
        b = qpe.at[quarter + i, :, z]
        return [
            rcopy(ref, ref, out_sem.at[12], e2_r.at[i], dev)
            for ref, dev in ((a, xid(1)), (b, zid(1)), (a, xid(3)), (b, zid(3)))
        ]

    def relay_pe(i):
        landed(qpe.at[i], e2_r.at[i])
        moves = (
            (qpe.at[i, xl, two[0]], xid(1)), (qpe.at[quarter + i, two[0], zl], zid(1)),
            (qpe.at[i, xr, two[1]], xid(3)), (qpe.at[quarter + i, two[1], zr], zid(3)),
        )
        start([rcopy(ref, ref, out_sem.at[13], e3_r.at[i], dev) for ref, dev in moves])

    def onward_pe_in(i):
        landed(qpe.at[i, pl.ds(0, 2)], e3_r.at[i])

    first = 4
    for i in range(first):
        start(near(i))

    more_routed.wait_recv()
    spread = dot(m0, ry[:, :, :lw].reshape(bl, lw))
    spread = jnp.where(lane // 64 == own, spread, 0.0).astype(BF16)
    fold = pick(iota((lw, 128), 0) % 64 == iota((lw, 128), 1) % 64)
    twice = dot(spread, fold)
    pairs = twice.reshape(half, 2, 16, 128)
    side = iota((half, 16, 128), 2) < 64
    qpe[:, x, z] = jnp.where(side, pairs[:, 0], pairs[:, 1]).astype(BF16)
    own_pe = twice[:, :64].astype(BF16)
    for i in range(0, first, 2):
        start(near_pe(i // 2))

    latrep[:, :lw] = dot(m1, ry[:, :, :lw].reshape(bl, lw)).astype(BF16)
    latrep[:, lw:] = dot(m1, ry[:, :, lw:].reshape(bl, 64)).astype(BF16)
    qo = qall[:, x, z].reshape(rows, lw)
    fresh = dot_nt(qo, latrep[:, :lw]) + dot_nt(own_pe, latrep[:, lw:])
    ri = iota((rows, rows), 0)
    ci = iota((rows, rows), 1)
    seen = (ri // 16 == ci // 16) & ((ci // 8) % 2 <= (ri // 8) % 2) & (ci % 8 == 0)
    fresh = jnp.where(seen, fresh * scale2, LOW)
    ftop = jnp.max(fresh, axis=1, keepdims=True)
    wf = jnp.where(seen, jnp.exp2(fresh - ftop), 0.0)
    fden = jnp.sum(wf, axis=1, keepdims=True)
    fnum = dot(wf.astype(BF16), latrep[:, :lw])

    def send(src, dst, ls, ld, n, rs, i, dev):
        return [
            rcopy(src, dst, out_sem.at[n], rs.at[0, i], dev),
            rcopy(ls, ld, out_sem.at[n + 1], rs.at[1, i], dev),
        ]

    def far(i):
        copies = []
        for j in range(2):
            a, b = pout.at[i, xo, two[j]], pout.at[half + i, two[j], zo]
            copies += send(a, h1.at[0, j, i], lrow.at[i, xo], lh1.at[0, j, i], 3, h_r, i,
                           xid(1 + 2 * j))
            copies += send(b, h1.at[1, j, i], lrow.at[half + i, zo], lh1.at[1, j, i], 3, h_r, i,
                           zid(1 + 2 * j))
        return copies

    def far_in(i):
        landed(pout.at[i, pl.ds(0, 2)], h_r.at[0, i])
        landed(lrow.at[i], h_r.at[1, i])

    last = half - 1

    def straight():
        a, b = pout.at[last, xo], pout.at[half + last, :, zo]
        return send(a, rd.at[0], lrow.at[last, xo], lrd.at[0], 3, h_r, last, xid(2)) + send(
            b, rd.at[1], lrow.at[half + last, zo], lrd.at[1], 3, h_r, last, zid(2))

    def straight_in():
        landed(rd, h_r.at[0, last])
        landed(lrd, h_r.at[1, last])

    def scatter1(i):
        copies = []
        for j in range(2):
            xt, zt = (xr, xl)[j], (zr, zl)[j]
            copies += send(pout.at[i, xt], r1.at[0, j, i], lrow.at[i, xt], lr1.at[0, j, i],
                           5, s1_r, i, xid(1 + 2 * j))
            copies += send(pout.at[half + i, :, zt], r1.at[1, j, i], lrow.at[half + i, zt],
                           lr1.at[1, j, i], 5, s1_r, i, zid(1 + 2 * j))
        return copies

    def scatter1_in(i):
        landed(pout.at[i], s1_r.at[0, i])
        landed(lrow.at[i], s1_r.at[1, i])

    def scatter2(i):
        copies = []
        for k in (1, 3, 2):
            copies += send(red1.at[0, i, lax.rem(z + k, NZ)], r2.at[0, k - 1, i], lred.at[0, i],
                           lr2.at[0, k - 1, i], 7, s2_r, i, zid(k))
            copies += send(red1.at[1, i, lax.rem(x + k, NX)], r2.at[1, k - 1, i], lred.at[1, i],
                           lr2.at[1, k - 1, i], 7, s2_r, i, xid(k))
        return copies

    def scatter2_in(i):
        landed(pout.at[i, pl.ds(0, 2), pl.ds(0, 3)], s2_r.at[0, i])
        landed(lrow.at[pl.ds(0, 2), pl.ds(0, 3)], s2_r.at[1, i])

    def weights(ls):
        top = functools.reduce(jnp.maximum, ls)
        ws = [jnp.exp2(v - top) for v in ls]
        total = functools.reduce(jnp.add, ws)
        inv = 1.0 / total
        return [w * inv for w in ws], top + jnp.log2(total)

    def column(w, n, off):
        shape = (n, 128)
        return jnp.sum(
            jnp.where(iota(shape, 1) == iota(shape, 0) + off, w, 0.0), axis=1, keepdims=True
        )

    def blend(blocks, ws, n, off):
        acc = 0.0
        for b, w in zip(blocks, ws):
            acc += column(w, n, off) * b.reshape(n, lw).astype(F32)
        return acc

    nq = 16 * NX * NZ
    row_q = iota((nq, 128), 0)
    lane_q = iota((nq, 128), 1)

    def attend(r, part):
        pltpu.make_async_copy(cache.at[r], cbuf.at[r], c_sem.at[r]).wait()
        q = qall[r].reshape(nq, lw)
        pair = qpe[r // 2].reshape(nq, 128)
        odd = jnp.full((1, 64), r % 2, F32).astype(BF16)
        pe = pair[:, :64] * (1.0 - odd) + pair[:, 64:] * odd
        c = cbuf.at[r]
        sc = dot(q, c[:lw, :]) + dot(pe, c[lw:, :])
        place = s * blk + iota((1, blk), 1)
        sc = sc + jnp.where(place < lens[g * nreq + r], 0.0, LOW)
        top = jnp.max(sc, axis=1, keepdims=True)
        w = jnp.exp2((sc - top) * scale2)
        den = jnp.sum(w, axis=1, keepdims=True)
        num = dot_nt(w.astype(BF16), c[:lw, :])
        pout[r] = (num * (1.0 / den)).astype(BF16).reshape(NX, NZ, 16, lw)
        lse = top * scale2 + jnp.log2(den)
        if part == 0:
            diag = jnp.where(lane_q == row_q % 64, lse, 0.0).reshape(4, 64, 128)
        else:
            diag = jnp.where(lane_q == row_q // 64 * 16 + row_q % 16, lse, 0.0)
            diag = jnp.sum(diag.reshape(4, 4, 16, 128), axis=0)
        for d in range(4):
            lrow[r, d] = jnp.sum(diag[d], axis=0, keepdims=True)

    lane_1 = iota((1, 128), 1)

    def middle(i):
        for j in range(2):
            xt, zt = (xr, xl)[j], (zr, zl)[j]
            keep = (lane_1 < 32) if j == 0 else (lane_1 >= 32)
            ws, ln = weights([lrow[i, xt], lh1[0, j, i]])
            acc = blend([pout[i, xt, two[j]], h1[0, j, i]], ws, 32, 32 * j)
            pout[i, xt, two[j]] = acc.astype(BF16).reshape(2, 16, lw)
            lrow[i, xt] = jnp.where(keep, ln, lrow[i, xt])
            r = half + i
            ws, ln = weights([lrow[r, zt], lh1[1, j, i]])
            acc = blend([pout[r, two[j], zt], h1[1, j, i]], ws, 32, 32 * j)
            pout[r, two[j], zt] = acc.astype(BF16).reshape(2, 16, lw)
            lrow[r, zt] = jnp.where(keep, ln, lrow[r, zt])

    def reduce1(i, more):
        ls = [lrow[i, x], lr1[0, 0, i], lr1[0, 1, i]] + ([lrd[0]] if more else [])
        blocks = [pout[i, x], r1[0, 0, i], r1[0, 1, i]] + ([rd[0]] if more else [])
        ws, ln = weights(ls)
        red1[0, i] = blend(blocks, ws, 64, 0).astype(BF16).reshape(4, 16, lw)
        lred[0, i] = ln
        r = half + i
        ls = [lrow[r, z], lr1[1, 0, i], lr1[1, 1, i]] + ([lrd[1]] if more else [])
        blocks = [pout[r, :, z], r1[1, 0, i], r1[1, 1, i]] + ([rd[1]] if more else [])
        ws, ln = weights(ls)
        red1[1, i] = blend(blocks, ws, 64, 0).astype(BF16).reshape(4, 16, lw)
        lred[1, i] = ln

    def reduce2(i):
        for part, own in ((0, z), (1, x)):
            ws, ln = weights([lred[part, i]] + [lr2[part, k, i] for k in range(3)])
            blocks = [red1[part, i, own]] + [r2[part, k, i] for k in range(3)]
            fin[part * half + i] = blend(blocks, ws, 16, own * 16)
            flse[part * half + i] = jnp.broadcast_to(column(ln, 16, own * 16), (16, 128))

    def step(t, carry):
        @pl.when(t + first < half)
        def _():
            start(near(t + first))

        @pl.when((t + first < half) & ((t + first) % 2 == 0))
        def _():
            start(near_pe((t + first) // 2))

        @pl.when(t < half)
        def _():
            near_in(t)
            start(direct(t))

        @pl.when((t < half) & (t % 2 == 0))
        def _():
            near_pe_in(t // 2)
            start(direct_pe(t // 2))

        i1 = t - 2

        @pl.when((i1 >= 0) & (i1 < half))
        def _():
            relay(i1)

        @pl.when((i1 >= 0) & (i1 < half) & (i1 % 2 == 0))
        def _():
            relay_pe(i1 // 2)

        i2 = t - 4

        @pl.when((i2 >= 0) & (i2 < half) & (i2 % 2 == 0))
        def _():
            onward_pe_in(i2 // 2)

        @pl.when((i2 >= 0) & (i2 < half))
        def _():
            onward_in(i2)
            attend(i2, 0)
            attend(half + i2, 1)

        @pl.when((i2 >= 0) & (i2 < last))
        def _():
            start(far(i2))

        @pl.when(i2 == last)
        def _():
            start(straight() + scatter1(last))

        i3 = t - 6

        @pl.when((i3 >= 0) & (i3 < last))
        def _():
            far_in(i3)
            middle(i3)
            start(scatter1(i3))

        i5 = t - 8

        @pl.when((i5 >= 0) & (i5 < last))
        def _():
            scatter1_in(i5)
            reduce1(i5, False)
            start(scatter2(i5))

        @pl.when(i5 == last)
        def _():
            scatter1_in(i5)
            straight_in()
            reduce1(i5, True)
            start(scatter2(i5))

        i7 = t - 10

        @pl.when(i7 >= 0)
        def _():
            scatter2_in(i7)
            reduce2(i7)

        return carry

    lax.fori_loop(0, half + 10, step, 0)

    w_copies[1].wait()
    lse = flse[...].reshape(rows, 128)[:, :1]
    top = jnp.maximum(ftop, lse)
    wc = jnp.exp2(lse - top)
    wn = jnp.exp2(ftop - top)
    den = wc + wn * fden
    num = wc * fin[...].reshape(rows, lw) + wn * fnum
    latent = (num * (1.0 / den)).astype(BF16)
    b0, b1 = [v.T.astype(BF16) for v in pulls]
    hrow = iota((rows, 128), 0) % 8
    for j in range(4):
        va0 = jnp.where(hrow == j, dot(latent, w_v[j]), 0.0).astype(BF16)
        vb0 = jnp.where(hrow == j + 4, dot(latent, w_v[j + 4]), 0.0).astype(BF16)
        back = dot(b0, va0) + dot(b1, vb0)
        tx2[:, :, j * 128 : (j + 1) * 128] = back.astype(BF16).reshape(ngrp, 16, 128)
        if j % 2 == 1:
            part = pl.ds((j - 1) * 128, 256)
            start([
                rcopy(tx2.at[d, :, part], rx2.at[g, :, part], out_sem.at[10], rb_r.at[0], {"grp": d})
                for d in dst
            ])

    rx2[g] = tx2[g]

    def left(ref, n):
        rcopy(ref, ref, out_sem.at[n], s1_r.at[0, 0], xid(1)).wait_send()

    left(qall.at[pl.ds(0, 3)], 0)
    left(qall.at[pl.ds(0, 8)], 1)
    left(qall.at[pl.ds(0, 4)], 2)
    left(pout.at[pl.ds(0, 4)], 3)
    left(lrow.at[pl.ds(0, 10), pl.ds(0, 3)], 4)
    left(pout.at[pl.ds(0, 8)], 5)
    left(lrow.at[pl.ds(0, 8)], 6)
    left(pout.at[pl.ds(0, 3)], 7)
    left(lrow.at[pl.ds(0, 12)], 8)
    left(qpe.at[pl.ds(0, 3), :, pl.ds(0, 2)], 11)
    left(qpe.at[pl.ds(0, 4)], 12)
    left(qpe.at[pl.ds(0, 2)], 13)
    all_routed.wait_send()
    more_routed.wait_send()
    all_home = rcopy(tx2.at[most], rx2.at[most], out_sem.at[10], rb_r.at[0], gid(1))
    all_home.wait_recv()
    got = rx2[...].reshape(bl, lw)
    for f in range(2):
        for t in range(2):
            kept = dot(sends[f][t].T.astype(BF16), got)
            out[pl.ds(t * nreq, nreq), pl.ds(f * lw, lw)] = kept.astype(BF16)

    all_home.wait_send()


def on_device(
    prefill_cache, lengths, decode_slots, q_nope, q_pe, new_latent, w_uk, value_up_weight
):
    ngrp = lax.axis_size("grp")
    nreq, blk, width = prefill_cache.shape
    steps = new_latent.shape[0]
    heads, nope, lw = w_uk.shape
    half = nreq // 2
    scale2 = (nope + width - lw) ** -0.5 * LOG2E

    rows = nreq * steps * heads
    vm = pl.BlockSpec(memory_space=pltpu.VMEM)
    dma = pltpu.SemaphoreType.DMA
    bytes_in = 2 * prefill_cache.size
    out = pl.pallas_call(
        functools.partial(kernel, ngrp, nreq, blk, scale2),
        out_shape=jax.ShapeDtypeStruct((steps * nreq, heads * 128), BF16),
        in_specs=[pl.BlockSpec(memory_space=pltpu.SMEM)] + [vm] * 4
        + [pl.BlockSpec(memory_space=pl.ANY)] * 3,
        out_specs=vm,
        scratch_shapes=[
            pltpu.VMEM((nreq, width, blk), BF16),
            pltpu.VMEM((heads * nope, lw), BF16),
            pltpu.VMEM((heads, lw, 128), BF16),
            pltpu.VMEM((ngrp, 16, lw), BF16),
            pltpu.VMEM((ngrp, 16, lw), BF16),
            pltpu.VMEM((ngrp, 16, width), BF16),
            pltpu.VMEM((ngrp, 16, width), BF16),
            pltpu.VMEM((rows, width), BF16),
            pltpu.VMEM((nreq, NX, NZ, 16, lw), BF16),
            pltpu.VMEM((half, NX, NZ, 16, 128), BF16),
            pltpu.VMEM((nreq, NX, NZ, 16, lw), BF16),
            pltpu.VMEM((nreq, 4, 1, 128), F32),
            pltpu.VMEM((2, 2, half, 2, 16, lw), BF16),
            pltpu.VMEM((2, 2, half, 1, 128), F32),
            pltpu.VMEM((2, 2, half, 4, 16, lw), BF16),
            pltpu.VMEM((2, 2, half, 1, 128), F32),
            pltpu.VMEM((2, 4, 16, lw), BF16),
            pltpu.VMEM((2, 1, 128), F32),
            pltpu.VMEM((2, half, 4, 16, lw), BF16),
            pltpu.VMEM((2, half, 1, 128), F32),
            pltpu.VMEM((2, 3, half, 16, lw), BF16),
            pltpu.VMEM((2, 3, half, 1, 128), F32),
            pltpu.VMEM((nreq, 16, lw), F32),
            pltpu.VMEM((nreq, 16, 128), F32),
            pltpu.VMEM((ngrp, 16, lw), BF16),
            pltpu.VMEM((ngrp, 16, lw), BF16),
            dma((nreq,)), dma((2,)), dma((15,)), dma((1,)), dma((1,)), dma((1,)),
            dma((half,)), dma((half,)), dma((half,)),
            dma((half // 2,)), dma((half // 2,)), dma((half // 2,)),
            dma((2, half)), dma((2, half)), dma((2, half)),
        ],
        compiler_params=pltpu.CompilerParams(
            collective_id=0, has_side_effects=True, vmem_limit_bytes=58 * 1024 * 1024
        ),
        cost_estimate=pl.CostEstimate(
            flops=2 * nreq * 256 * blk * (width + lw), bytes_accessed=bytes_in,
            transcendentals=nreq * 256 * blk,
        ),
    )(
        lengths, decode_slots,
        q_nope.reshape(steps * nreq, -1), q_pe.reshape(steps * nreq, -1),
        new_latent.reshape(steps * nreq, -1), w_uk.reshape(heads * nope, lw),
        value_up_weight, jnp.swapaxes(prefill_cache, 1, 2),
    )
    return out.reshape(steps, nreq, -1)


def solution(mesh):
    return jax.shard_map(
        on_device,
        mesh=mesh,
        in_specs=(
            P("grp", "seq", None),
            P(),
            P(),
            P(None, "grp", "seq"),
            P(None, "grp", "seq"),
            P(None, "grp", None),
            P("seq", None, None),
            P("seq", None, None),
        ),
        out_specs=P(None, "grp", "seq"),
        check_vma=False,
    )
```

```python
import functools

import jax
import jax.numpy as jnp
from jax import lax
from jax.experimental import pallas as pl
from jax.experimental.pallas import tpu as pltpu
from jax.sharding import PartitionSpec as P

MESH = pl.DeviceIdType.MESH
LOG2E = 1.4426950408889634
LOW = -1e30
CAP = 3
NX = 4
NZ = 4
F32 = jnp.float32
BF16 = jnp.bfloat16


def dot(a, b):
    return jnp.dot(a, b, preferred_element_type=F32)


def dot_nt(a, b):
    return lax.dot_general(a, b, (((1,), (1,)), ((), ())), preferred_element_type=F32)


def iota(shape, dim):
    return lax.broadcasted_iota(jnp.int32, shape, dim)


def pick(cond):
    return jnp.where(cond, 1.0, 0.0).astype(BF16)


def kernel(
    ngrp, nreq, blk, scale2,
    lens, slots, qn, qp, lat, w_uk_hbm, w_v_hbm, cache,
    out,
    cbuf, w_uk, w_v, tx, rx, ty, ry, latrep, qall, qpe, pout, lrow, h1, lh1, r1, lr1, rd, lrd, red1, lred, h2, lh2, lred2, r2, lr2,
    fin, flse, tx2, rx2,
    c_sem, w_sem, out_sem, rt_r, ru_r, rb_r, g0_r, g1_r, g2_r, g3_r, e1_r, e2_r, e3_r, h_r, s1_r, h2_r, s2_r,
):
    g = lax.axis_index("grp")
    s = lax.axis_index("seq")
    x = lax.div(s, NZ)
    z = lax.rem(s, NZ)
    half = nreq // 2
    rows = nreq * 16
    lw = 512
    c_copies = [pltpu.make_async_copy(cache.at[r], cbuf.at[r], c_sem.at[r]) for r in range(nreq)]
    w_copies = [
        pltpu.make_async_copy(w_uk_hbm, w_uk, w_sem.at[0]),
        pltpu.make_async_copy(w_v_hbm, w_v, w_sem.at[1]),
    ]
    for c in w_copies + c_copies:
        c.start()

    def gid(k):
        return {"grp": lax.rem(g + k, ngrp)}

    def xid(k):
        return {"seq": lax.rem(x + k, NX) * NZ + z}

    def zid(k):
        return {"seq": x * NZ + lax.rem(z + k, NZ)}

    def rcopy(src, dst, ss, rs, dev):
        return pltpu.make_async_remote_copy(
            src_ref=src, dst_ref=dst, send_sem=ss, recv_sem=rs, device_id=dev, device_id_type=MESH
        )

    barrier = pltpu.get_barrier_semaphore()
    for k in range(1, ngrp):
        pl.semaphore_signal(barrier, inc=1, device_id=gid(k), device_id_type=MESH)
    for k in range(1, 4):
        pl.semaphore_signal(barrier, inc=1, device_id=xid(k), device_id_type=MESH)
        pl.semaphore_signal(barrier, inc=1, device_id=zid(k), device_id_type=MESH)

    shift = nreq.bit_length() - 1
    served = slots[...]
    dest = lax.shift_right_logical(served, shift)
    lane_s = iota((ngrp, nreq), 1)
    rank = jnp.zeros((ngrp, nreq), jnp.int32)
    for j in range(nreq - 1):
        rank += jnp.where((dest == dest[:, j : j + 1]) & (lane_s > j), 1, 0)
    origin = iota((ngrp, nreq), 0) * 16 + 2 * rank
    mine = iota((ngrp, nreq), 0) == g
    rho = jnp.sum(jnp.where(mine, dest * 16 + 2 * rank, 0), axis=0, keepdims=True)
    row_id = iota((rows, nreq), 0)
    asked = g * nreq + row_id // 16
    sig = jnp.zeros((rows, nreq), jnp.int32)
    for j in range(ngrp):
        sig += jnp.where(served[j : j + 1, :] == asked, origin[j : j + 1, :], 0)
    sig = jnp.sum(sig, axis=1, keepdims=True) + (iota((rows, 1), 0) // 8) % 2

    bl = ngrp * 16
    row_l = iota((bl, nreq), 0)
    sends = [[jnp.where(row_l == rho + t + 2 * CAP * f, 1.0, 0.0) for t in range(2)] for f in range(2)]

    def send_dot(f, cols):
        both = [dot(sends[f][t].astype(BF16), cols(pl.ds(t * nreq, nreq))) for t in range(2)]
        return both[0] + both[1]

    head = send_dot(0, lambda r: qn[r, :lw]) + send_dot(1, lambda r: qn[r, lw:])
    tx[...] = head.astype(BF16).reshape(ngrp, 16, lw)
    mid = send_dot(0, lambda r: qp[r, :]) + send_dot(1, lambda r: lat[r, :lw])
    ty[:, :, :lw] = mid.astype(BF16).reshape(ngrp, 16, lw)
    tail = send_dot(1, lambda r: lat[r, lw:])
    ty[:, :, lw:] = tail.astype(BF16).reshape(ngrp, 16, 64)
    pl.semaphore_wait(barrier, ngrp - 1 + 6)
    dst = [lax.rem(g + k, ngrp) for k in range(1, ngrp)]
    route = [
        rcopy(tx.at[d], rx.at[g], out_sem.at[9], rt_r.at[0], {"grp": d}) for d in dst
    ] + [
        rcopy(ty.at[d], ry.at[g], out_sem.at[14], ru_r.at[0], {"grp": d}) for d in dst
    ]
    for c in route:
        c.start()
    rx[g] = tx[g]
    ry[g] = ty[g]
    most = pl.ds(0, ngrp - 1)
    all_routed = rcopy(tx.at[most], rx.at[most], out_sem.at[9], rt_r.at[0], gid(1))
    more_routed = rcopy(ty.at[most], ry.at[most], out_sem.at[14], ru_r.at[0], gid(1))
    all_routed.wait_recv()

    col_l = iota((rows, bl), 1)
    pulls = [jnp.where(col_l == sig + 2 * CAP * f, 1.0, 0.0) for f in range(2)]
    m0, m1 = [v.astype(BF16) for v in pulls]
    own = iota((rows, lw), 0) % 8
    lane = iota((rows, lw), 1)
    w_copies[0].wait()
    absorbed = jnp.zeros((rows, lw), F32)
    for j in range(2):
        spread = dot((m0, m1)[j], rx[...].reshape(bl, lw))
        spread = jnp.where(lane // 128 + 4 * j == own, spread, 0.0).astype(BF16)
        absorbed += dot(spread, w_uk[j * lw : (j + 1) * lw, :])
    qall[:, x, z] = absorbed.astype(BF16).reshape(nreq, 16, lw)
    xl = lax.rem(x + 3, NX)
    xr = lax.rem(x + 1, NX)
    xo = lax.rem(x + 2, NX)
    zl = lax.rem(z + 3, NZ)
    zr = lax.rem(z + 1, NZ)
    zo = lax.rem(z + 2, NZ)
    two = (pl.ds(0, 2), pl.ds(2, 2))

    def start(copies):
        for c in copies:
            c.start()

    def landed(ref, sem):
        rcopy(ref, ref, out_sem.at[0], sem, xid(1)).wait_recv()

    def near(i, hops):
        copies = []
        for k in hops:
            a, b = qall.at[i, x, z], qall.at[half + i, x, z]
            copies.append(rcopy(a, a, out_sem.at[0], g1_r.at[i], zid(k)))
            copies.append(rcopy(b, b, out_sem.at[0], g1_r.at[i], xid(k)))
        return copies

    straight_steps = 2

    def pass_on(i):
        landed(qall.at[i, 0], g1_r.at[i])
        turn = 2 * (i % 2)
        a = qall.at[i, x, lax.rem(z + 3 + turn, NZ)]
        b = qall.at[half + i, lax.rem(x + 3 + turn, NX), z]
        rcopy(a, a, out_sem.at[0], g0_r.at[i], zid(1 + turn)).start()
        rcopy(b, b, out_sem.at[0], g0_r.at[i], xid(1 + turn)).start()

    def direct(i):
        a = qall.at[i, x]
        b = qall.at[half + i, :, z]
        return [
            rcopy(ref, ref, out_sem.at[1], g2_r.at[i], dev)
            for ref, dev in ((a, xid(1)), (b, zid(1)), (a, xid(3)), (b, zid(3)))
        ]

    def direct_in(i):
        landed(qall.at[i], g2_r.at[i])

    def onward(i):
        moves = (
            (qall.at[i, xl, two[0]], xid(1)), (qall.at[half + i, two[0], zl], zid(1)),
            (qall.at[i, xr, two[1]], xid(3)), (qall.at[half + i, two[1], zr], zid(3)),
        )
        return [rcopy(ref, ref, out_sem.at[2], g3_r.at[i], dev) for ref, dev in moves]

    def onward_in(i):
        landed(qall.at[i, pl.ds(0, 2)], g3_r.at[i])

    def relay(i):
        direct_in(i)
        start(onward(i))

    quarter = half // 2

    def near_pe(i):
        copies = []
        for k in (1, 3, 2):
            a, b = qpe.at[i, x, z], qpe.at[quarter + i, x, z]
            copies.append(rcopy(a, a, out_sem.at[11], e1_r.at[i], zid(k)))
            copies.append(rcopy(b, b, out_sem.at[11], e1_r.at[i], xid(k)))
        return copies

    def near_pe_in(i):
        landed(qpe.at[i, pl.ds(0, 2), pl.ds(0, 3)], e1_r.at[i])

    def direct_pe(i):
        a = qpe.at[i, x]
        b = qpe.at[quarter + i, :, z]
        return [
            rcopy(ref, ref, out_sem.at[12], e2_r.at[i], dev)
            for ref, dev in ((a, xid(1)), (b, zid(1)), (a, xid(3)), (b, zid(3)))
        ]

    def relay_pe(i):
        landed(qpe.at[i], e2_r.at[i])
        moves = (
            (qpe.at[i, xl, two[0]], xid(1)), (qpe.at[quarter + i, two[0], zl], zid(1)),
            (qpe.at[i, xr, two[1]], xid(3)), (qpe.at[quarter + i, two[1], zr], zid(3)),
        )
        start([rcopy(ref, ref, out_sem.at[13], e3_r.at[i], dev) for ref, dev in moves])

    def onward_pe_in(i):
        landed(qpe.at[i, pl.ds(0, 2)], e3_r.at[i])

    first = 4
    for i in range(first):
        start(near(i, (1, 3, 2) if i < straight_steps else (1, 3)))

    more_routed.wait_recv()
    spread = dot(m0, ry[:, :, :lw].reshape(bl, lw))
    spread = jnp.where(lane // 64 == own, spread, 0.0).astype(BF16)
    fold = pick(iota((lw, 128), 0) % 64 == iota((lw, 128), 1) % 64)
    twice = dot(spread, fold)
    pairs = twice.reshape(half, 2, 16, 128)
    side = iota((half, 16, 128), 2) < 64
    qpe[:, x, z] = jnp.where(side, pairs[:, 0], pairs[:, 1]).astype(BF16)
    own_pe = twice[:, :64].astype(BF16)
    for i in range(0, first, 2):
        start(near_pe(i // 2))

    latrep[:, :lw] = dot(m1, ry[:, :, :lw].reshape(bl, lw)).astype(BF16)
    latrep[:, lw:] = dot(m1, ry[:, :, lw:].reshape(bl, 64)).astype(BF16)
    qo = qall[:, x, z].reshape(rows, lw)
    fresh = dot_nt(qo, latrep[:, :lw]) + dot_nt(own_pe, latrep[:, lw:])
    ri = iota((rows, rows), 0)
    ci = iota((rows, rows), 1)
    seen = (ri // 16 == ci // 16) & ((ci // 8) % 2 <= (ri // 8) % 2) & (ci % 8 == 0)
    fresh = jnp.where(seen, fresh * scale2, LOW)
    ftop = jnp.max(fresh, axis=1, keepdims=True)
    wf = jnp.where(seen, jnp.exp2(fresh - ftop), 0.0)
    fden = jnp.sum(wf, axis=1, keepdims=True)
    fnum = dot(wf.astype(BF16), latrep[:, :lw])

    def send(src, dst, ls, ld, n, rs, i, dev):
        return [
            rcopy(src, dst, out_sem.at[n], rs.at[0, i], dev),
            rcopy(ls, ld, out_sem.at[n + 1], rs.at[1, i], dev),
        ]

    def far(i):
        copies = []
        for j in range(2):
            a, b = pout.at[i, xo, two[j]], pout.at[half + i, two[j], zo]
            copies += send(a, h1.at[0, j, i], lrow.at[i, xo], lh1.at[0, j, i], 3, h_r, i,
                           xid(1 + 2 * j))
            copies += send(b, h1.at[1, j, i], lrow.at[half + i, zo], lh1.at[1, j, i], 3, h_r, i,
                           zid(1 + 2 * j))
        return copies

    def far_in(i):
        landed(pout.at[i, pl.ds(0, 2)], h_r.at[0, i])
        landed(lrow.at[i], h_r.at[1, i])

    last = half - 1

    def straight():
        a, b = pout.at[last, xo], pout.at[half + last, :, zo]
        return send(a, rd.at[0], lrow.at[last, xo], lrd.at[0], 3, h_r, last, xid(2)) + send(
            b, rd.at[1], lrow.at[half + last, zo], lrd.at[1], 3, h_r, last, zid(2))

    def straight_in():
        landed(rd, h_r.at[0, last])
        landed(lrd, h_r.at[1, last])

    def scatter1(i):
        copies = []
        for j in range(2):
            xt, zt = (xr, xl)[j], (zr, zl)[j]
            copies += send(pout.at[i, xt], r1.at[0, j, i], lrow.at[i, xt], lr1.at[0, j, i],
                           5, s1_r, i, xid(1 + 2 * j))
            copies += send(pout.at[half + i, :, zt], r1.at[1, j, i], lrow.at[half + i, zt],
                           lr1.at[1, j, i], 5, s1_r, i, zid(1 + 2 * j))
        return copies

    def scatter1_in(i):
        landed(pout.at[i], s1_r.at[0, i])
        landed(lrow.at[i], s1_r.at[1, i])

    def far2(i):
        turn = 2 * (i % 2)
        return send(red1.at[0, i, zo], h2.at[0, i], lred.at[0, i], lh2.at[0, i], 15, h2_r, i,
                    zid(1 + turn)) + send(
            red1.at[1, i, xo], h2.at[1, i], lred.at[1, i], lh2.at[1, i], 15, h2_r, i,
            xid(1 + turn))

    def far2_in(i):
        landed(pout.at[i, 0, pl.ds(0, 2)], h2_r.at[0, i])
        landed(lrow.at[i, pl.ds(0, 2)], h2_r.at[1, i])

    def scatter2(i):
        copies = []
        for j in range(2):
            xt, zt = (xr, xl)[j], (zr, zl)[j]
            copies += send(red1.at[0, i, zt], r2.at[0, j, i], lred2.at[0, i], lr2.at[0, j, i],
                           7, s2_r, i, zid(1 + 2 * j))
            copies += send(red1.at[1, i, xt], r2.at[1, j, i], lred2.at[1, i], lr2.at[1, j, i],
                           7, s2_r, i, xid(1 + 2 * j))
        return copies

    def scatter2_in(i):
        landed(pout.at[i, 0], s2_r.at[0, i])
        landed(lrow.at[i], s2_r.at[1, i])

    def straight2():
        copies = []
        for k in (1, 3, 2):
            copies += send(red1.at[0, last, lax.rem(z + k, NZ)], r2.at[0, k - 1, last],
                           lred.at[0, last], lr2.at[0, k - 1, last], 17, s2_r, last, zid(k))
            copies += send(red1.at[1, last, lax.rem(x + k, NX)], r2.at[1, k - 1, last],
                           lred.at[1, last], lr2.at[1, k - 1, last], 17, s2_r, last, xid(k))
        return copies

    def straight2_in():
        landed(pout.at[last, pl.ds(0, 2), pl.ds(0, 3)], s2_r.at[0, last])
        landed(lrow.at[pl.ds(0, 2), pl.ds(0, 3)], s2_r.at[1, last])

    def weights(ls):
        top = functools.reduce(jnp.maximum, ls)
        ws = [jnp.exp2(v - top) for v in ls]
        total = functools.reduce(jnp.add, ws)
        inv = 1.0 / total
        return [w * inv for w in ws], top + jnp.log2(total)

    def column(w, n, off):
        shape = (n, 128)
        return jnp.sum(
            jnp.where(iota(shape, 1) == iota(shape, 0) + off, w, 0.0), axis=1, keepdims=True
        )

    def blend(blocks, ws, n, off):
        acc = 0.0
        for b, w in zip(blocks, ws):
            acc += column(w, n, off) * b.reshape(n, lw).astype(F32)
        return acc

    nq = 16 * NX * NZ
    row_q = iota((nq, 128), 0)
    lane_q = iota((nq, 128), 1)

    def attend(r, part):
        pltpu.make_async_copy(cache.at[r], cbuf.at[r], c_sem.at[r]).wait()
        q = qall[r].reshape(nq, lw)
        pair = qpe[r // 2].reshape(nq, 128)
        odd = jnp.full((1, 64), r % 2, F32).astype(BF16)
        pe = pair[:, :64] * (1.0 - odd) + pair[:, 64:] * odd
        c = cbuf.at[r]
        sc = dot(q, c[:lw, :]) + dot(pe, c[lw:, :])
        place = s * blk + iota((1, blk), 1)
        sc = sc + jnp.where(place < lens[g * nreq + r], 0.0, LOW)
        top = jnp.max(sc, axis=1, keepdims=True)
        w = jnp.exp2((sc - top) * scale2)
        den = jnp.sum(w, axis=1, keepdims=True)
        num = dot_nt(w.astype(BF16), c[:lw, :])
        pout[r] = (num * (1.0 / den)).astype(BF16).reshape(NX, NZ, 16, lw)
        lse = top * scale2 + jnp.log2(den)
        if part == 0:
            diag = jnp.where(lane_q == row_q % 64, lse, 0.0).reshape(4, 64, 128)
        else:
            diag = jnp.where(lane_q == row_q // 64 * 16 + row_q % 16, lse, 0.0)
            diag = jnp.sum(diag.reshape(4, 4, 16, 128), axis=0)
        for d in range(4):
            lrow[r, d] = jnp.sum(diag[d], axis=0, keepdims=True)

    lane_1 = iota((1, 128), 1)

    def middle(i):
        for j in range(2):
            xt, zt = (xr, xl)[j], (zr, zl)[j]
            keep = (lane_1 < 32) if j == 0 else (lane_1 >= 32)
            ws, ln = weights([lrow[i, xt], lh1[0, j, i]])
            acc = blend([pout[i, xt, two[j]], h1[0, j, i]], ws, 32, 32 * j)
            pout[i, xt, two[j]] = acc.astype(BF16).reshape(2, 16, lw)
            lrow[i, xt] = jnp.where(keep, ln, lrow[i, xt])
            r = half + i
            ws, ln = weights([lrow[r, zt], lh1[1, j, i]])
            acc = blend([pout[r, two[j], zt], h1[1, j, i]], ws, 32, 32 * j)
            pout[r, two[j], zt] = acc.astype(BF16).reshape(2, 16, lw)
            lrow[r, zt] = jnp.where(keep, ln, lrow[r, zt])

    def reduce1(i, more):
        ls = [lrow[i, x], lr1[0, 0, i], lr1[0, 1, i]] + ([lrd[0]] if more else [])
        blocks = [pout[i, x], r1[0, 0, i], r1[0, 1, i]] + ([rd[0]] if more else [])
        ws, ln = weights(ls)
        red1[0, i] = blend(blocks, ws, 64, 0).astype(BF16).reshape(4, 16, lw)
        lred[0, i] = ln
        r = half + i
        ls = [lrow[r, z], lr1[1, 0, i], lr1[1, 1, i]] + ([lrd[1]] if more else [])
        blocks = [pout[r, :, z], r1[1, 0, i], r1[1, 1, i]] + ([rd[1]] if more else [])
        ws, ln = weights(ls)
        red1[1, i] = blend(blocks, ws, 64, 0).astype(BF16).reshape(4, 16, lw)
        lred[1, i] = ln

    def middle2(i):
        turn = 2 * (i % 2)
        for part, own in ((0, z), (1, x)):
            to = lax.rem(own + 1 + turn, 4)
            ws, ln = weights([lred[part, i], lh2[part, i]])
            acc = blend([red1[part, i, to], h2[part, i]], ws, 16, to * 16)
            red1[part, i, to] = acc.astype(BF16)
            lred2[part, i] = jnp.where(lane_1 // 16 == to, ln, lred[part, i])

    def reduce2(i, n):
        for part, own in ((0, z), (1, x)):
            ws, ln = weights([lred[part, i]] + [lr2[part, k, i] for k in range(n)])
            blocks = [red1[part, i, own]] + [r2[part, k, i] for k in range(n)]
            fin[part * half + i] = blend(blocks, ws, 16, own * 16)
            flse[part * half + i] = jnp.broadcast_to(column(ln, 16, own * 16), (16, 128))

    def step(t, carry):
        @pl.when(t + first < half)
        def _():
            start(near(t + first, (1, 3)))

        @pl.when((t + first < half) & ((t + first) % 2 == 0))
        def _():
            start(near_pe((t + first) // 2))

        @pl.when(t < straight_steps)
        def _():
            landed(qall.at[t, pl.ds(0, 2), pl.ds(0, 3)], g1_r.at[t])

        @pl.when((t >= straight_steps) & (t < half))
        def _():
            landed(qall.at[t, 0, pl.ds(0, 2)], g0_r.at[t])

        @pl.when(t < half)
        def _():
            start(direct(t))

        @pl.when(t + straight_steps < half)
        def _():
            pass_on(t + straight_steps)

        @pl.when((t < half) & (t % 2 == 0))
        def _():
            near_pe_in(t // 2)
            start(direct_pe(t // 2))

        i1 = t - 2

        @pl.when((i1 >= 0) & (i1 < half))
        def _():
            relay(i1)

        @pl.when((i1 >= 0) & (i1 < half) & (i1 % 2 == 0))
        def _():
            relay_pe(i1 // 2)

        i2 = t - 4

        @pl.when((i2 >= 0) & (i2 < half) & (i2 % 2 == 0))
        def _():
            onward_pe_in(i2 // 2)

        @pl.when((i2 >= 0) & (i2 < half))
        def _():
            onward_in(i2)
            attend(i2, 0)
            attend(half + i2, 1)

        @pl.when((i2 >= 0) & (i2 < last))
        def _():
            start(far(i2))

        @pl.when(i2 == last)
        def _():
            start(straight() + scatter1(last))

        i3 = t - 6

        @pl.when((i3 >= 0) & (i3 < last))
        def _():
            far_in(i3)
            middle(i3)
            start(scatter1(i3))

        i5 = t - 8

        @pl.when((i5 >= 0) & (i5 < last))
        def _():
            scatter1_in(i5)
            reduce1(i5, False)
            start(far2(i5))

        @pl.when(i5 == last)
        def _():
            scatter1_in(i5)
            straight_in()
            reduce1(i5, True)
            start(straight2())

        i6 = t - 9

        @pl.when((i6 >= 0) & (i6 < last))
        def _():
            far2_in(i6)
            middle2(i6)
            start(scatter2(i6))

        i7 = t - 11

        @pl.when((i7 >= 0) & (i7 < last))
        def _():
            scatter2_in(i7)
            reduce2(i7, 2)

        @pl.when(i7 == last)
        def _():
            straight2_in()
            reduce2(last, 3)

        return carry

    lax.fori_loop(0, half + 11, step, 0)

    w_copies[1].wait()
    lse = flse[...].reshape(rows, 128)[:, :1]
    top = jnp.maximum(ftop, lse)
    wc = jnp.exp2(lse - top)
    wn = jnp.exp2(ftop - top)
    den = wc + wn * fden
    num = wc * fin[...].reshape(rows, lw) + wn * fnum
    latent = (num * (1.0 / den)).astype(BF16)
    b0, b1 = [v.T.astype(BF16) for v in pulls]
    hrow = iota((rows, 128), 0) % 8
    for j in range(4):
        va0 = jnp.where(hrow == j, dot(latent, w_v[j]), 0.0).astype(BF16)
        vb0 = jnp.where(hrow == j + 4, dot(latent, w_v[j + 4]), 0.0).astype(BF16)
        back = dot(b0, va0) + dot(b1, vb0)
        tx2[:, :, j * 128 : (j + 1) * 128] = back.astype(BF16).reshape(ngrp, 16, 128)
        if j % 2 == 1:
            part = pl.ds((j - 1) * 128, 256)
            start([
                rcopy(tx2.at[d, :, part], rx2.at[g, :, part], out_sem.at[10], rb_r.at[0], {"grp": d})
                for d in dst
            ])

    rx2[g] = tx2[g]

    def left(ref, n):
        rcopy(ref, ref, out_sem.at[n], s1_r.at[0, 0], xid(1)).wait_send()

    left(qall.at[pl.ds(0, 3)], 0)
    left(qall.at[pl.ds(0, 8)], 1)
    left(qall.at[pl.ds(0, 4)], 2)
    left(pout.at[pl.ds(0, 4)], 3)
    left(lrow.at[pl.ds(0, 10), pl.ds(0, 3)], 4)
    left(pout.at[pl.ds(0, 8)], 5)
    left(lrow.at[pl.ds(0, 8)], 6)
    left(pout.at[pl.ds(0, 7), 0], 7)
    left(lrow.at[pl.ds(0, 7)], 8)
    left(pout.at[pl.ds(0, 7), 0, pl.ds(0, 2)], 15)
    left(lrow.at[pl.ds(0, 7), pl.ds(0, 2)], 16)
    left(pout.at[0, pl.ds(0, 2), pl.ds(0, 3)], 17)
    left(lrow.at[pl.ds(0, 2), pl.ds(0, 3)], 18)
    left(qpe.at[pl.ds(0, 3), :, pl.ds(0, 2)], 11)
    left(qpe.at[pl.ds(0, 4)], 12)
    left(qpe.at[pl.ds(0, 2)], 13)
    all_routed.wait_send()
    more_routed.wait_send()
    all_home = rcopy(tx2.at[most], rx2.at[most], out_sem.at[10], rb_r.at[0], gid(1))
    all_home.wait_recv()
    got = rx2[...].reshape(bl, lw)
    for f in range(2):
        for t in range(2):
            kept = dot(sends[f][t].T.astype(BF16), got)
            out[pl.ds(t * nreq, nreq), pl.ds(f * lw, lw)] = kept.astype(BF16)

    all_home.wait_send()


def on_device(
    prefill_cache, lengths, decode_slots, q_nope, q_pe, new_latent, w_uk, value_up_weight
):
    ngrp = lax.axis_size("grp")
    nreq, blk, width = prefill_cache.shape
    steps = new_latent.shape[0]
    heads, nope, lw = w_uk.shape
    half = nreq // 2
    scale2 = (nope + width - lw) ** -0.5 * LOG2E

    rows = nreq * steps * heads
    vm = pl.BlockSpec(memory_space=pltpu.VMEM)
    dma = pltpu.SemaphoreType.DMA
    bytes_in = 2 * prefill_cache.size
    out = pl.pallas_call(
        functools.partial(kernel, ngrp, nreq, blk, scale2),
        out_shape=jax.ShapeDtypeStruct((steps * nreq, heads * 128), BF16),
        in_specs=[pl.BlockSpec(memory_space=pltpu.SMEM)] + [vm] * 4
        + [pl.BlockSpec(memory_space=pl.ANY)] * 3,
        out_specs=vm,
        scratch_shapes=[
            pltpu.VMEM((nreq, width, blk), BF16),
            pltpu.VMEM((heads * nope, lw), BF16),
            pltpu.VMEM((heads, lw, 128), BF16),
            pltpu.VMEM((ngrp, 16, lw), BF16),
            pltpu.VMEM((ngrp, 16, lw), BF16),
            pltpu.VMEM((ngrp, 16, width), BF16),
            pltpu.VMEM((ngrp, 16, width), BF16),
            pltpu.VMEM((rows, width), BF16),
            pltpu.VMEM((nreq, NX, NZ, 16, lw), BF16),
            pltpu.VMEM((half, NX, NZ, 16, 128), BF16),
            pltpu.VMEM((nreq, NX, NZ, 16, lw), BF16),
            pltpu.VMEM((nreq, 4, 1, 128), F32),
            pltpu.VMEM((2, 2, half, 2, 16, lw), BF16),
            pltpu.VMEM((2, 2, half, 1, 128), F32),
            pltpu.VMEM((2, 2, half, 4, 16, lw), BF16),
            pltpu.VMEM((2, 2, half, 1, 128), F32),
            pltpu.VMEM((2, 4, 16, lw), BF16),
            pltpu.VMEM((2, 1, 128), F32),
            pltpu.VMEM((2, half, 4, 16, lw), BF16),
            pltpu.VMEM((2, half, 1, 128), F32),
            pltpu.VMEM((2, half, 16, lw), BF16),
            pltpu.VMEM((2, half, 1, 128), F32),
            pltpu.VMEM((2, half, 1, 128), F32),
            pltpu.VMEM((2, 3, half, 16, lw), BF16),
            pltpu.VMEM((2, 3, half, 1, 128), F32),
            pltpu.VMEM((nreq, 16, lw), F32),
            pltpu.VMEM((nreq, 16, 128), F32),
            pltpu.VMEM((ngrp, 16, lw), BF16),
            pltpu.VMEM((ngrp, 16, lw), BF16),
            dma((nreq,)), dma((2,)), dma((19,)), dma((1,)), dma((1,)), dma((1,)),
            dma((half,)), dma((half,)), dma((half,)), dma((half,)),
            dma((half // 2,)), dma((half // 2,)), dma((half // 2,)),
            dma((2, half)), dma((2, half)), dma((2, half)), dma((2, half)),
        ],
        compiler_params=pltpu.CompilerParams(
            collective_id=0, has_side_effects=True, vmem_limit_bytes=58 * 1024 * 1024
        ),
        cost_estimate=pl.CostEstimate(
            flops=2 * nreq * 256 * blk * (width + lw), bytes_accessed=bytes_in,
            transcendentals=nreq * 256 * blk,
        ),
    )(
        lengths, decode_slots,
        q_nope.reshape(steps * nreq, -1), q_pe.reshape(steps * nreq, -1),
        new_latent.reshape(steps * nreq, -1), w_uk.reshape(heads * nope, lw),
        value_up_weight, jnp.swapaxes(prefill_cache, 1, 2),
    )
    return out.reshape(steps, nreq, -1)


def solution(mesh):
    return jax.shard_map(
        on_device,
        mesh=mesh,
        in_specs=(
            P("grp", "seq", None),
            P(),
            P(),
            P(None, "grp", "seq"),
            P(None, "grp", "seq"),
            P(None, "grp", None),
            P("seq", None, None),
            P("seq", None, None),
        ),
        out_specs=P(None, "grp", "seq"),
        check_vma=False,
    )
```

```python
import functools

import jax
import jax.numpy as jnp
from jax import lax
from jax.experimental import pallas as pl
from jax.experimental.pallas import tpu as pltpu
from jax.sharding import PartitionSpec as P

MESH = pl.DeviceIdType.MESH
LOG2E = 1.4426950408889634
LOW = -1e30
CAP = 3
NX = 4
NZ = 4
F32 = jnp.float32
BF16 = jnp.bfloat16


def dot(a, b):
    return jnp.dot(a, b, preferred_element_type=F32)


def dot_nt(a, b):
    return lax.dot_general(a, b, (((1,), (1,)), ((), ())), preferred_element_type=F32)


def iota(shape, dim):
    return lax.broadcasted_iota(jnp.int32, shape, dim)


def pick(cond):
    return jnp.where(cond, 1.0, 0.0).astype(BF16)


def kernel(
    ngrp, nreq, blk, scale2,
    lens, slots, qn, qp, lat, w_uk_hbm, w_v_hbm, cache,
    out,
    cbuf, w_uk, w_v, tx, rx, ty, ry, latrep, qall, qpe, pout, lrow, h1, lh1, r1, lr1, rd, lrd, red1, lred, r2, lr2,
    fin, flse, tx2, rx2,
    c_sem, w_sem, out_sem, rt_r, ru_r, rb_r, g0_r, g1_r, g2_r, g3_r, e1_r, e2_r, e3_r, h_r, s1_r, s2_r,
):
    g = lax.axis_index("grp")
    s = lax.axis_index("seq")
    x = lax.div(s, NZ)
    z = lax.rem(s, NZ)
    half = nreq // 2
    rows = nreq * 16
    lw = 512
    c_copies = [pltpu.make_async_copy(cache.at[r], cbuf.at[r], c_sem.at[r]) for r in range(nreq)]
    w_copies = [
        pltpu.make_async_copy(w_uk_hbm, w_uk, w_sem.at[0]),
        pltpu.make_async_copy(w_v_hbm, w_v, w_sem.at[1]),
    ]
    for c in w_copies + c_copies:
        c.start()

    def gid(k):
        return {"grp": lax.rem(g + k, ngrp)}

    def xid(k):
        return {"seq": lax.rem(x + k, NX) * NZ + z}

    def zid(k):
        return {"seq": x * NZ + lax.rem(z + k, NZ)}

    def rcopy(src, dst, ss, rs, dev):
        return pltpu.make_async_remote_copy(
            src_ref=src, dst_ref=dst, send_sem=ss, recv_sem=rs, device_id=dev, device_id_type=MESH
        )

    barrier = pltpu.get_barrier_semaphore()
    for k in range(1, ngrp):
        pl.semaphore_signal(barrier, inc=1, device_id=gid(k), device_id_type=MESH)
    for k in range(1, 4):
        pl.semaphore_signal(barrier, inc=1, device_id=xid(k), device_id_type=MESH)
        pl.semaphore_signal(barrier, inc=1, device_id=zid(k), device_id_type=MESH)

    shift = nreq.bit_length() - 1
    served = slots[...]
    dest = lax.shift_right_logical(served, shift)
    lane_s = iota((ngrp, nreq), 1)
    rank = jnp.zeros((ngrp, nreq), jnp.int32)
    for j in range(nreq - 1):
        rank += jnp.where((dest == dest[:, j : j + 1]) & (lane_s > j), 1, 0)
    origin = iota((ngrp, nreq), 0) * 16 + 2 * rank
    mine = iota((ngrp, nreq), 0) == g
    rho = jnp.sum(jnp.where(mine, dest * 16 + 2 * rank, 0), axis=0, keepdims=True)
    row_id = iota((rows, nreq), 0)
    asked = g * nreq + row_id // 16
    sig = jnp.zeros((rows, nreq), jnp.int32)
    for j in range(ngrp):
        sig += jnp.where(served[j : j + 1, :] == asked, origin[j : j + 1, :], 0)
    sig = jnp.sum(sig, axis=1, keepdims=True) + (iota((rows, 1), 0) // 8) % 2

    bl = ngrp * 16
    row_l = iota((bl, nreq), 0)
    sends = [[jnp.where(row_l == rho + t + 2 * CAP * f, 1.0, 0.0) for t in range(2)] for f in range(2)]

    def send_dot(f, cols):
        both = [dot(sends[f][t].astype(BF16), cols(pl.ds(t * nreq, nreq))) for t in range(2)]
        return both[0] + both[1]

    head = send_dot(0, lambda r: qn[r, :lw]) + send_dot(1, lambda r: qn[r, lw:])
    tx[...] = head.astype(BF16).reshape(ngrp, 16, lw)
    mid = send_dot(0, lambda r: qp[r, :]) + send_dot(1, lambda r: lat[r, :lw])
    ty[:, :, :lw] = mid.astype(BF16).reshape(ngrp, 16, lw)
    tail = send_dot(1, lambda r: lat[r, lw:])
    ty[:, :, lw:] = tail.astype(BF16).reshape(ngrp, 16, 64)
    pl.semaphore_wait(barrier, ngrp - 1 + 6)
    dst = [lax.rem(g + k, ngrp) for k in range(1, ngrp)]
    route = [
        rcopy(tx.at[d], rx.at[g], out_sem.at[9], rt_r.at[0], {"grp": d}) for d in dst
    ] + [
        rcopy(ty.at[d], ry.at[g], out_sem.at[14], ru_r.at[0], {"grp": d}) for d in dst
    ]
    for c in route:
        c.start()
    rx[g] = tx[g]
    ry[g] = ty[g]
    most = pl.ds(0, ngrp - 1)
    all_routed = rcopy(tx.at[most], rx.at[most], out_sem.at[9], rt_r.at[0], gid(1))
    more_routed = rcopy(ty.at[most], ry.at[most], out_sem.at[14], ru_r.at[0], gid(1))
    all_routed.wait_recv()

    col_l = iota((rows, bl), 1)
    pulls = [jnp.where(col_l == sig + 2 * CAP * f, 1.0, 0.0) for f in range(2)]
    m0, m1 = [v.astype(BF16) for v in pulls]
    own = iota((rows, lw), 0) % 8
    lane = iota((rows, lw), 1)
    w_copies[0].wait()
    absorbed = jnp.zeros((rows, lw), F32)
    for j in range(2):
        spread = dot((m0, m1)[j], rx[...].reshape(bl, lw))
        spread = jnp.where(lane // 128 + 4 * j == own, spread, 0.0).astype(BF16)
        absorbed += dot(spread, w_uk[j * lw : (j + 1) * lw, :])
    qall[:, x, z] = absorbed.astype(BF16).reshape(nreq, 16, lw)
    xl = lax.rem(x + 3, NX)
    xr = lax.rem(x + 1, NX)
    xo = lax.rem(x + 2, NX)
    zl = lax.rem(z + 3, NZ)
    zr = lax.rem(z + 1, NZ)
    zo = lax.rem(z + 2, NZ)
    two = (pl.ds(0, 2), pl.ds(2, 2))

    def start(copies):
        for c in copies:
            c.start()

    def landed(ref, sem):
        rcopy(ref, ref, out_sem.at[0], sem, xid(1)).wait_recv()

    def near(i, hops):
        copies = []
        for k in hops:
            a, b = qall.at[i, x, z], qall.at[half + i, x, z]
            copies.append(rcopy(a, a, out_sem.at[0], g1_r.at[i], zid(k)))
            copies.append(rcopy(b, b, out_sem.at[0], g1_r.at[i], xid(k)))
        return copies

    straight_steps = 2

    def pass_on(i):
        landed(qall.at[i, 0], g1_r.at[i])
        turn = 2 * (i % 2)
        a = qall.at[i, x, lax.rem(z + 3 + turn, NZ)]
        b = qall.at[half + i, lax.rem(x + 3 + turn, NX), z]
        rcopy(a, a, out_sem.at[0], g0_r.at[i], zid(1 + turn)).start()
        rcopy(b, b, out_sem.at[0], g0_r.at[i], xid(1 + turn)).start()

    def direct(i):
        a = qall.at[i, x]
        b = qall.at[half + i, :, z]
        return [
            rcopy(ref, ref, out_sem.at[1], g2_r.at[i], dev)
            for ref, dev in ((a, xid(1)), (b, zid(1)), (a, xid(3)), (b, zid(3)))
        ]

    def direct_in(i):
        landed(qall.at[i], g2_r.at[i])

    def onward(i):
        moves = (
            (qall.at[i, xl, two[0]], xid(1)), (qall.at[half + i, two[0], zl], zid(1)),
            (qall.at[i, xr, two[1]], xid(3)), (qall.at[half + i, two[1], zr], zid(3)),
        )
        return [rcopy(ref, ref, out_sem.at[2], g3_r.at[i], dev) for ref, dev in moves]

    def onward_in(i):
        landed(qall.at[i, pl.ds(0, 2)], g3_r.at[i])

    def relay(i):
        direct_in(i)
        start(onward(i))

    quarter = half // 2

    def near_pe(i):
        copies = []
        for k in (1, 3, 2):
            a, b = qpe.at[i, x, z], qpe.at[quarter + i, x, z]
            copies.append(rcopy(a, a, out_sem.at[11], e1_r.at[i], zid(k)))
            copies.append(rcopy(b, b, out_sem.at[11], e1_r.at[i], xid(k)))
        return copies

    def near_pe_in(i):
        landed(qpe.at[i, pl.ds(0, 2), pl.ds(0, 3)], e1_r.at[i])

    def direct_pe(i):
        a = qpe.at[i, x]
        b = qpe.at[quarter + i, :, z]
        return [
            rcopy(ref, ref, out_sem.at[12], e2_r.at[i], dev)
            for ref, dev in ((a, xid(1)), (b, zid(1)), (a, xid(3)), (b, zid(3)))
        ]

    def relay_pe(i):
        landed(qpe.at[i], e2_r.at[i])
        moves = (
            (qpe.at[i, xl, two[0]], xid(1)), (qpe.at[quarter + i, two[0], zl], zid(1)),
            (qpe.at[i, xr, two[1]], xid(3)), (qpe.at[quarter + i, two[1], zr], zid(3)),
        )
        start([rcopy(ref, ref, out_sem.at[13], e3_r.at[i], dev) for ref, dev in moves])

    def onward_pe_in(i):
        landed(qpe.at[i, pl.ds(0, 2)], e3_r.at[i])

    first = 4
    for i in range(first):
        start(near(i, (1, 3, 2) if i < straight_steps else (1, 3)))

    more_routed.wait_recv()
    spread = dot(m0, ry[:, :, :lw].reshape(bl, lw))
    spread = jnp.where(lane // 64 == own, spread, 0.0).astype(BF16)
    fold = pick(iota((lw, 128), 0) % 64 == iota((lw, 128), 1) % 64)
    twice = dot(spread, fold)
    pairs = twice.reshape(half, 2, 16, 128)
    side = iota((half, 16, 128), 2) < 64
    qpe[:, x, z] = jnp.where(side, pairs[:, 0], pairs[:, 1]).astype(BF16)
    own_pe = twice[:, :64].astype(BF16)
    for i in range(0, first, 2):
        start(near_pe(i // 2))

    latrep[:, :lw] = dot(m1, ry[:, :, :lw].reshape(bl, lw)).astype(BF16)
    latrep[:, lw:] = dot(m1, ry[:, :, lw:].reshape(bl, 64)).astype(BF16)
    qo = qall[:, x, z].reshape(rows, lw)
    fresh = dot_nt(qo, latrep[:, :lw]) + dot_nt(own_pe, latrep[:, lw:])
    ri = iota((rows, rows), 0)
    ci = iota((rows, rows), 1)
    seen = (ri // 16 == ci // 16) & ((ci // 8) % 2 <= (ri // 8) % 2) & (ci % 8 == 0)
    fresh = jnp.where(seen, fresh * scale2, LOW)
    ftop = jnp.max(fresh, axis=1, keepdims=True)
    wf = jnp.where(seen, jnp.exp2(fresh - ftop), 0.0)
    fden = jnp.sum(wf, axis=1, keepdims=True)
    fnum = dot(wf.astype(BF16), latrep[:, :lw])

    def send(src, dst, ls, ld, n, rs, i, dev):
        return [
            rcopy(src, dst, out_sem.at[n], rs.at[0, i], dev),
            rcopy(ls, ld, out_sem.at[n + 1], rs.at[1, i], dev),
        ]

    def far(i):
        copies = []
        for j in range(2):
            a, b = pout.at[i, xo, two[j]], pout.at[half + i, two[j], zo]
            copies += send(a, h1.at[0, j, i], lrow.at[i, xo], lh1.at[0, j, i], 3, h_r, i,
                           xid(1 + 2 * j))
            copies += send(b, h1.at[1, j, i], lrow.at[half + i, zo], lh1.at[1, j, i], 3, h_r, i,
                           zid(1 + 2 * j))
        return copies

    def far_in(i):
        landed(pout.at[i, pl.ds(0, 2)], h_r.at[0, i])
        landed(lrow.at[i], h_r.at[1, i])

    last = half - 1

    def straight():
        a, b = pout.at[last, xo], pout.at[half + last, :, zo]
        return send(a, rd.at[0], lrow.at[last, xo], lrd.at[0], 3, h_r, last, xid(2)) + send(
            b, rd.at[1], lrow.at[half + last, zo], lrd.at[1], 3, h_r, last, zid(2))

    def straight_in():
        landed(rd, h_r.at[0, last])
        landed(lrd, h_r.at[1, last])

    def scatter1(i):
        copies = []
        for j in range(2):
            xt, zt = (xr, xl)[j], (zr, zl)[j]
            copies += send(pout.at[i, xt], r1.at[0, j, i], lrow.at[i, xt], lr1.at[0, j, i],
                           5, s1_r, i, xid(1 + 2 * j))
            copies += send(pout.at[half + i, :, zt], r1.at[1, j, i], lrow.at[half + i, zt],
                           lr1.at[1, j, i], 5, s1_r, i, zid(1 + 2 * j))
        return copies

    def scatter1_in(i):
        landed(pout.at[i], s1_r.at[0, i])
        landed(lrow.at[i], s1_r.at[1, i])

    def scatter2(i):
        copies = []
        for k in (1, 3, 2):
            copies += send(red1.at[0, i, lax.rem(z + k, NZ)], r2.at[0, k - 1, i], lred.at[0, i],
                           lr2.at[0, k - 1, i], 7, s2_r, i, zid(k))
            copies += send(red1.at[1, i, lax.rem(x + k, NX)], r2.at[1, k - 1, i], lred.at[1, i],
                           lr2.at[1, k - 1, i], 7, s2_r, i, xid(k))
        return copies

    def scatter2_in(i):
        landed(pout.at[i, pl.ds(0, 2), pl.ds(0, 3)], s2_r.at[0, i])
        landed(lrow.at[pl.ds(0, 2), pl.ds(0, 3)], s2_r.at[1, i])

    def weights(ls):
        top = functools.reduce(jnp.maximum, ls)
        ws = [jnp.exp2(v - top) for v in ls]
        total = functools.reduce(jnp.add, ws)
        inv = 1.0 / total
        return [w * inv for w in ws], top + jnp.log2(total)

    def column(w, n, off):
        shape = (n, 128)
        return jnp.sum(
            jnp.where(iota(shape, 1) == iota(shape, 0) + off, w, 0.0), axis=1, keepdims=True
        )

    def blend(blocks, ws, n, off):
        acc = 0.0
        for b, w in zip(blocks, ws):
            acc += column(w, n, off) * b.reshape(n, lw).astype(F32)
        return acc

    nq = 16 * NX * NZ
    row_q = iota((nq, 128), 0)
    lane_q = iota((nq, 128), 1)

    def attend(r, part):
        pltpu.make_async_copy(cache.at[r], cbuf.at[r], c_sem.at[r]).wait()
        q = qall[r].reshape(nq, lw)
        pair = qpe[r // 2].reshape(nq, 128)
        odd = jnp.full((1, 64), r % 2, F32).astype(BF16)
        pe = pair[:, :64] * (1.0 - odd) + pair[:, 64:] * odd
        c = cbuf.at[r]
        sc = dot(q, c[:lw, :]) + dot(pe, c[lw:, :])
        place = s * blk + iota((1, blk), 1)
        sc = sc + jnp.where(place < lens[g * nreq + r], 0.0, LOW)
        top = jnp.max(sc, axis=1, keepdims=True)
        w = jnp.exp2((sc - top) * scale2)
        den = jnp.sum(w, axis=1, keepdims=True)
        num = dot_nt(w.astype(BF16), c[:lw, :])
        pout[r] = (num * (1.0 / den)).astype(BF16).reshape(NX, NZ, 16, lw)
        lse = top * scale2 + jnp.log2(den)
        if part == 0:
            diag = jnp.where(lane_q == row_q % 64, lse, 0.0).reshape(4, 64, 128)
        else:
            diag = jnp.where(lane_q == row_q // 64 * 16 + row_q % 16, lse, 0.0)
            diag = jnp.sum(diag.reshape(4, 4, 16, 128), axis=0)
        for d in range(4):
            lrow[r, d] = jnp.sum(diag[d], axis=0, keepdims=True)

    lane_1 = iota((1, 128), 1)

    def middle(i):
        for j in range(2):
            xt, zt = (xr, xl)[j], (zr, zl)[j]
            keep = (lane_1 < 32) if j == 0 else (lane_1 >= 32)
            ws, ln = weights([lrow[i, xt], lh1[0, j, i]])
            acc = blend([pout[i, xt, two[j]], h1[0, j, i]], ws, 32, 32 * j)
            pout[i, xt, two[j]] = acc.astype(BF16).reshape(2, 16, lw)
            lrow[i, xt] = jnp.where(keep, ln, lrow[i, xt])
            r = half + i
            ws, ln = weights([lrow[r, zt], lh1[1, j, i]])
            acc = blend([pout[r, two[j], zt], h1[1, j, i]], ws, 32, 32 * j)
            pout[r, two[j], zt] = acc.astype(BF16).reshape(2, 16, lw)
            lrow[r, zt] = jnp.where(keep, ln, lrow[r, zt])

    def reduce1(i, more):
        ls = [lrow[i, x], lr1[0, 0, i], lr1[0, 1, i]] + ([lrd[0]] if more else [])
        blocks = [pout[i, x], r1[0, 0, i], r1[0, 1, i]] + ([rd[0]] if more else [])
        ws, ln = weights(ls)
        red1[0, i] = blend(blocks, ws, 64, 0).astype(BF16).reshape(4, 16, lw)
        lred[0, i] = ln
        r = half + i
        ls = [lrow[r, z], lr1[1, 0, i], lr1[1, 1, i]] + ([lrd[1]] if more else [])
        blocks = [pout[r, :, z], r1[1, 0, i], r1[1, 1, i]] + ([rd[1]] if more else [])
        ws, ln = weights(ls)
        red1[1, i] = blend(blocks, ws, 64, 0).astype(BF16).reshape(4, 16, lw)
        lred[1, i] = ln

    def reduce2(i):
        for part, own in ((0, z), (1, x)):
            ws, ln = weights([lred[part, i]] + [lr2[part, k, i] for k in range(3)])
            blocks = [red1[part, i, own]] + [r2[part, k, i] for k in range(3)]
            fin[part * half + i] = blend(blocks, ws, 16, own * 16)
            flse[part * half + i] = jnp.broadcast_to(column(ln, 16, own * 16), (16, 128))

    def step(t, carry):
        @pl.when(t + first < half)
        def _():
            start(near(t + first, (1, 3)))

        @pl.when((t + first < half) & ((t + first) % 2 == 0))
        def _():
            start(near_pe((t + first) // 2))

        @pl.when(t < straight_steps)
        def _():
            landed(qall.at[t, pl.ds(0, 2), pl.ds(0, 3)], g1_r.at[t])

        @pl.when((t >= straight_steps) & (t < half))
        def _():
            landed(qall.at[t, 0, pl.ds(0, 2)], g0_r.at[t])

        @pl.when(t < half)
        def _():
            start(direct(t))

        @pl.when(t + straight_steps < half)
        def _():
            pass_on(t + straight_steps)

        @pl.when((t < half) & (t % 2 == 0))
        def _():
            near_pe_in(t // 2)
            start(direct_pe(t // 2))

        i1 = t - 2

        @pl.when((i1 >= 0) & (i1 < half))
        def _():
            relay(i1)

        @pl.when((i1 >= 0) & (i1 < half) & (i1 % 2 == 0))
        def _():
            relay_pe(i1 // 2)

        i2 = t - 4

        @pl.when((i2 >= 0) & (i2 < half) & (i2 % 2 == 0))
        def _():
            onward_pe_in(i2 // 2)

        @pl.when((i2 >= 0) & (i2 < half))
        def _():
            onward_in(i2)
            attend(i2, 0)
            attend(half + i2, 1)

        @pl.when((i2 >= 0) & (i2 < last))
        def _():
            start(far(i2))

        @pl.when(i2 == last)
        def _():
            start(straight() + scatter1(last))

        i3 = t - 6

        @pl.when((i3 >= 0) & (i3 < last))
        def _():
            far_in(i3)
            middle(i3)
            start(scatter1(i3))

        i5 = t - 9

        @pl.when((i5 >= 0) & (i5 < last))
        def _():
            scatter1_in(i5)
            reduce1(i5, False)
            start(scatter2(i5))

        @pl.when(i5 == last)
        def _():
            scatter1_in(i5)
            straight_in()
            reduce1(i5, True)
            start(scatter2(i5))

        i7 = t - 12

        @pl.when(i7 >= 0)
        def _():
            scatter2_in(i7)
            reduce2(i7)

        return carry

    lax.fori_loop(0, half + 12, step, 0)

    w_copies[1].wait()
    lse = flse[...].reshape(rows, 128)[:, :1]
    top = jnp.maximum(ftop, lse)
    wc = jnp.exp2(lse - top)
    wn = jnp.exp2(ftop - top)
    den = wc + wn * fden
    num = wc * fin[...].reshape(rows, lw) + wn * fnum
    latent = (num * (1.0 / den)).astype(BF16)
    b0, b1 = [v.T.astype(BF16) for v in pulls]
    hrow = iota((rows, 128), 0) % 8
    for j in range(4):
        va0 = jnp.where(hrow == j, dot(latent, w_v[j]), 0.0).astype(BF16)
        vb0 = jnp.where(hrow == j + 4, dot(latent, w_v[j + 4]), 0.0).astype(BF16)
        back = dot(b0, va0) + dot(b1, vb0)
        tx2[:, :, j * 128 : (j + 1) * 128] = back.astype(BF16).reshape(ngrp, 16, 128)
        if j % 2 == 1:
            part = pl.ds((j - 1) * 128, 256)
            start([
                rcopy(tx2.at[d, :, part], rx2.at[g, :, part], out_sem.at[10], rb_r.at[0], {"grp": d})
                for d in dst
            ])

    rx2[g] = tx2[g]

    def left(ref, n):
        rcopy(ref, ref, out_sem.at[n], s1_r.at[0, 0], xid(1)).wait_send()

    left(qall.at[pl.ds(0, 3)], 0)
    left(qall.at[pl.ds(0, 8)], 1)
    left(qall.at[pl.ds(0, 4)], 2)
    left(pout.at[pl.ds(0, 4)], 3)
    left(lrow.at[pl.ds(0, 10), pl.ds(0, 3)], 4)
    left(pout.at[pl.ds(0, 8)], 5)
    left(lrow.at[pl.ds(0, 8)], 6)
    left(pout.at[pl.ds(0, 3)], 7)
    left(lrow.at[pl.ds(0, 12)], 8)
    left(qpe.at[pl.ds(0, 3), :, pl.ds(0, 2)], 11)
    left(qpe.at[pl.ds(0, 4)], 12)
    left(qpe.at[pl.ds(0, 2)], 13)
    all_routed.wait_send()
    more_routed.wait_send()
    all_home = rcopy(tx2.at[most], rx2.at[most], out_sem.at[10], rb_r.at[0], gid(1))
    all_home.wait_recv()
    got = rx2[...].reshape(bl, lw)
    for f in range(2):
        for t in range(2):
            kept = dot(sends[f][t].T.astype(BF16), got)
            out[pl.ds(t * nreq, nreq), pl.ds(f * lw, lw)] = kept.astype(BF16)

    all_home.wait_send()


def on_device(
    prefill_cache, lengths, decode_slots, q_nope, q_pe, new_latent, w_uk, value_up_weight
):
    ngrp = lax.axis_size("grp")
    nreq, blk, width = prefill_cache.shape
    steps = new_latent.shape[0]
    heads, nope, lw = w_uk.shape
    half = nreq // 2
    scale2 = (nope + width - lw) ** -0.5 * LOG2E

    rows = nreq * steps * heads
    vm = pl.BlockSpec(memory_space=pltpu.VMEM)
    dma = pltpu.SemaphoreType.DMA
    bytes_in = 2 * prefill_cache.size
    out = pl.pallas_call(
        functools.partial(kernel, ngrp, nreq, blk, scale2),
        out_shape=jax.ShapeDtypeStruct((steps * nreq, heads * 128), BF16),
        in_specs=[pl.BlockSpec(memory_space=pltpu.SMEM)] + [vm] * 4
        + [pl.BlockSpec(memory_space=pl.ANY)] * 3,
        out_specs=vm,
        scratch_shapes=[
            pltpu.VMEM((nreq, width, blk), BF16),
            pltpu.VMEM((heads * nope, lw), BF16),
            pltpu.VMEM((heads, lw, 128), BF16),
            pltpu.VMEM((ngrp, 16, lw), BF16),
            pltpu.VMEM((ngrp, 16, lw), BF16),
            pltpu.VMEM((ngrp, 16, width), BF16),
            pltpu.VMEM((ngrp, 16, width), BF16),
            pltpu.VMEM((rows, width), BF16),
            pltpu.VMEM((nreq, NX, NZ, 16, lw), BF16),
            pltpu.VMEM((half, NX, NZ, 16, 128), BF16),
            pltpu.VMEM((nreq, NX, NZ, 16, lw), BF16),
            pltpu.VMEM((nreq, 4, 1, 128), F32),
            pltpu.VMEM((2, 2, half, 2, 16, lw), BF16),
            pltpu.VMEM((2, 2, half, 1, 128), F32),
            pltpu.VMEM((2, 2, half, 4, 16, lw), BF16),
            pltpu.VMEM((2, 2, half, 1, 128), F32),
            pltpu.VMEM((2, 4, 16, lw), BF16),
            pltpu.VMEM((2, 1, 128), F32),
            pltpu.VMEM((2, half, 4, 16, lw), BF16),
            pltpu.VMEM((2, half, 1, 128), F32),
            pltpu.VMEM((2, 3, half, 16, lw), BF16),
            pltpu.VMEM((2, 3, half, 1, 128), F32),
            pltpu.VMEM((nreq, 16, lw), F32),
            pltpu.VMEM((nreq, 16, 128), F32),
            pltpu.VMEM((ngrp, 16, lw), BF16),
            pltpu.VMEM((ngrp, 16, lw), BF16),
            dma((nreq,)), dma((2,)), dma((15,)), dma((1,)), dma((1,)), dma((1,)),
            dma((half,)), dma((half,)), dma((half,)), dma((half,)),
            dma((half // 2,)), dma((half // 2,)), dma((half // 2,)),
            dma((2, half)), dma((2, half)), dma((2, half)),
        ],
        compiler_params=pltpu.CompilerParams(
            collective_id=0, has_side_effects=True, vmem_limit_bytes=58 * 1024 * 1024
        ),
        cost_estimate=pl.CostEstimate(
            flops=2 * nreq * 256 * blk * (width + lw), bytes_accessed=bytes_in,
            transcendentals=nreq * 256 * blk,
        ),
    )(
        lengths, decode_slots,
        q_nope.reshape(steps * nreq, -1), q_pe.reshape(steps * nreq, -1),
        new_latent.reshape(steps * nreq, -1), w_uk.reshape(heads * nope, lw),
        value_up_weight, jnp.swapaxes(prefill_cache, 1, 2),
    )
    return out.reshape(steps, nreq, -1)


def solution(mesh):
    return jax.shard_map(
        on_device,
        mesh=mesh,
        in_specs=(
            P("grp", "seq", None),
            P(),
            P(),
            P(None, "grp", "seq"),
            P(None, "grp", "seq"),
            P(None, "grp", None),
            P("seq", None, None),
            P("seq", None, None),
        ),
        out_specs=P(None, "grp", "seq"),
        check_vma=False,
    )
```

```python
import functools

import jax
import jax.numpy as jnp
from jax import lax
from jax.experimental import pallas as pl
from jax.experimental.pallas import tpu as pltpu
from jax.sharding import PartitionSpec as P

MESH = pl.DeviceIdType.MESH
LOG2E = 1.4426950408889634
LOW = -1e30
CAP = 3
NX = 4
NZ = 4
F32 = jnp.float32
BF16 = jnp.bfloat16


def dot(a, b):
    return jnp.dot(a, b, preferred_element_type=F32)


def dot_nt(a, b):
    return lax.dot_general(a, b, (((1,), (1,)), ((), ())), preferred_element_type=F32)


def iota(shape, dim):
    return lax.broadcasted_iota(jnp.int32, shape, dim)


def pick(cond):
    return jnp.where(cond, 1.0, 0.0).astype(BF16)


def kernel(
    ngrp, nreq, blk, scale2,
    lens, slots, qn, qp, lat, w_uk_hbm, w_v_hbm, cache,
    out,
    cbuf, w_uk, w_v, tx, rx, ty, ry, latrep, qall, qpe, pout, lrow, h1, lh1, r1, lr1, rd, lrd, red1, lred, r2, lr2,
    fin, flse, early, tx2, rx2,
    c_sem, w_sem, out_sem, rt_r, ru_r, rb_r, g0_r, g1_r, g2_r, g3_r, e1_r, e2_r, e3_r, h_r, s1_r, s2_r,
):
    g = lax.axis_index("grp")
    s = lax.axis_index("seq")
    x = lax.div(s, NZ)
    z = lax.rem(s, NZ)
    half = nreq // 2
    rows = nreq * 16
    lw = 512
    c_copies = [pltpu.make_async_copy(cache.at[r], cbuf.at[r], c_sem.at[r]) for r in range(nreq)]
    w_copies = [
        pltpu.make_async_copy(w_uk_hbm, w_uk, w_sem.at[0]),
        pltpu.make_async_copy(w_v_hbm, w_v, w_sem.at[1]),
    ]
    for c in w_copies + c_copies:
        c.start()

    def gid(k):
        return {"grp": lax.rem(g + k, ngrp)}

    def xid(k):
        return {"seq": lax.rem(x + k, NX) * NZ + z}

    def zid(k):
        return {"seq": x * NZ + lax.rem(z + k, NZ)}

    def rcopy(src, dst, ss, rs, dev):
        return pltpu.make_async_remote_copy(
            src_ref=src, dst_ref=dst, send_sem=ss, recv_sem=rs, device_id=dev, device_id_type=MESH
        )

    barrier = pltpu.get_barrier_semaphore()
    for k in range(1, ngrp):
        pl.semaphore_signal(barrier, inc=1, device_id=gid(k), device_id_type=MESH)
    for k in range(1, 4):
        pl.semaphore_signal(barrier, inc=1, device_id=xid(k), device_id_type=MESH)
        pl.semaphore_signal(barrier, inc=1, device_id=zid(k), device_id_type=MESH)

    shift = nreq.bit_length() - 1
    served = slots[...]
    dest = lax.shift_right_logical(served, shift)
    lane_s = iota((ngrp, nreq), 1)
    rank = jnp.zeros((ngrp, nreq), jnp.int32)
    for j in range(nreq - 1):
        rank += jnp.where((dest == dest[:, j : j + 1]) & (lane_s > j), 1, 0)
    origin = iota((ngrp, nreq), 0) * 16 + 2 * rank
    mine = iota((ngrp, nreq), 0) == g
    rho = jnp.sum(jnp.where(mine, dest * 16 + 2 * rank, 0), axis=0, keepdims=True)
    row_id = iota((rows, nreq), 0)
    asked = g * nreq + row_id // 16
    sig = jnp.zeros((rows, nreq), jnp.int32)
    for j in range(ngrp):
        sig += jnp.where(served[j : j + 1, :] == asked, origin[j : j + 1, :], 0)
    sig = jnp.sum(sig, axis=1, keepdims=True) + (iota((rows, 1), 0) // 8) % 2

    bl = ngrp * 16
    row_l = iota((bl, nreq), 0)
    sends = [[jnp.where(row_l == rho + t + 2 * CAP * f, 1.0, 0.0) for t in range(2)] for f in range(2)]

    def send_dot(f, cols):
        both = [dot(sends[f][t].astype(BF16), cols(pl.ds(t * nreq, nreq))) for t in range(2)]
        return both[0] + both[1]

    head = send_dot(0, lambda r: qn[r, :lw]) + send_dot(1, lambda r: qn[r, lw:])
    tx[...] = head.astype(BF16).reshape(ngrp, 16, lw)
    mid = send_dot(0, lambda r: qp[r, :]) + send_dot(1, lambda r: lat[r, :lw])
    ty[:, :, :lw] = mid.astype(BF16).reshape(ngrp, 16, lw)
    tail = send_dot(1, lambda r: lat[r, lw:])
    ty[:, :, lw:] = tail.astype(BF16).reshape(ngrp, 16, 64)
    pl.semaphore_wait(barrier, ngrp - 1 + 6)
    dst = [lax.rem(g + k, ngrp) for k in range(1, ngrp)]
    route = [
        rcopy(tx.at[d], rx.at[g], out_sem.at[9], rt_r.at[0], {"grp": d}) for d in dst
    ] + [
        rcopy(ty.at[d], ry.at[g], out_sem.at[14], ru_r.at[0], {"grp": d}) for d in dst
    ]
    for c in route:
        c.start()
    rx[g] = tx[g]
    ry[g] = ty[g]
    most = pl.ds(0, ngrp - 1)
    all_routed = rcopy(tx.at[most], rx.at[most], out_sem.at[9], rt_r.at[0], gid(1))
    more_routed = rcopy(ty.at[most], ry.at[most], out_sem.at[14], ru_r.at[0], gid(1))
    col_l = iota((rows, bl), 1)
    pulls = [jnp.where(col_l == sig + 2 * CAP * f, 1.0, 0.0) for f in range(2)]
    m0, m1 = [v.astype(BF16) for v in pulls]
    own = iota((rows, lw), 0) % 8
    lane = iota((rows, lw), 1)
    def part_of(v, h):
        n = rows // 4
        return jnp.concatenate([v[n * h : n * h + n], v[n * h + 2 * n : n * h + 3 * n]], axis=0)

    backs = [[part_of(v, h).T.astype(BF16) for v in pulls] for h in range(2)]
    keeps = [[sends[f][t].T.astype(BF16) for t in range(2)] for f in range(2)]
    all_routed.wait_recv()

    w_copies[0].wait()
    absorbed = jnp.zeros((rows, lw), F32)
    for j in range(2):
        spread = dot((m0, m1)[j], rx[...].reshape(bl, lw))
        spread = jnp.where(lane // 128 + 4 * j == own, spread, 0.0).astype(BF16)
        absorbed += dot(spread, w_uk[j * lw : (j + 1) * lw, :])
    qall[:, x, z] = absorbed.astype(BF16).reshape(nreq, 16, lw)
    xl = lax.rem(x + 3, NX)
    xr = lax.rem(x + 1, NX)
    xo = lax.rem(x + 2, NX)
    zl = lax.rem(z + 3, NZ)
    zr = lax.rem(z + 1, NZ)
    zo = lax.rem(z + 2, NZ)
    two = (pl.ds(0, 2), pl.ds(2, 2))

    def start(copies):
        for c in copies:
            c.start()

    def landed(ref, sem):
        rcopy(ref, ref, out_sem.at[0], sem, xid(1)).wait_recv()

    def near(i, hops):
        copies = []
        for k in hops:
            a, b = qall.at[i, x, z], qall.at[half + i, x, z]
            copies.append(rcopy(a, a, out_sem.at[0], g1_r.at[i], zid(k)))
            copies.append(rcopy(b, b, out_sem.at[0], g1_r.at[i], xid(k)))
        return copies

    straight_steps = 2

    def pass_on(i):
        landed(qall.at[i, 0], g1_r.at[i])
        turn = 2 * (i % 2)
        a = qall.at[i, x, lax.rem(z + 3 + turn, NZ)]
        b = qall.at[half + i, lax.rem(x + 3 + turn, NX), z]
        rcopy(a, a, out_sem.at[0], g0_r.at[i], zid(1 + turn)).start()
        rcopy(b, b, out_sem.at[0], g0_r.at[i], xid(1 + turn)).start()

    def direct(i):
        a = qall.at[i, x]
        b = qall.at[half + i, :, z]
        return [
            rcopy(ref, ref, out_sem.at[1], g2_r.at[i], dev)
            for ref, dev in ((a, xid(1)), (b, zid(1)), (a, xid(3)), (b, zid(3)))
        ]

    def direct_in(i):
        landed(qall.at[i], g2_r.at[i])

    def onward(i):
        moves = (
            (qall.at[i, xl, two[0]], xid(1)), (qall.at[half + i, two[0], zl], zid(1)),
            (qall.at[i, xr, two[1]], xid(3)), (qall.at[half + i, two[1], zr], zid(3)),
        )
        return [rcopy(ref, ref, out_sem.at[2], g3_r.at[i], dev) for ref, dev in moves]

    def onward_in(i):
        landed(qall.at[i, pl.ds(0, 2)], g3_r.at[i])

    def relay(i):
        direct_in(i)
        start(onward(i))

    quarter = half // 2

    def near_pe(i):
        copies = []
        for k in (1, 3, 2):
            a, b = qpe.at[i, x, z], qpe.at[quarter + i, x, z]
            copies.append(rcopy(a, a, out_sem.at[11], e1_r.at[i], zid(k)))
            copies.append(rcopy(b, b, out_sem.at[11], e1_r.at[i], xid(k)))
        return copies

    def near_pe_in(i):
        landed(qpe.at[i, pl.ds(0, 2), pl.ds(0, 3)], e1_r.at[i])

    def direct_pe(i):
        a = qpe.at[i, x]
        b = qpe.at[quarter + i, :, z]
        return [
            rcopy(ref, ref, out_sem.at[12], e2_r.at[i], dev)
            for ref, dev in ((a, xid(1)), (b, zid(1)), (a, xid(3)), (b, zid(3)))
        ]

    def relay_pe(i):
        landed(qpe.at[i], e2_r.at[i])
        moves = (
            (qpe.at[i, xl, two[0]], xid(1)), (qpe.at[quarter + i, two[0], zl], zid(1)),
            (qpe.at[i, xr, two[1]], xid(3)), (qpe.at[quarter + i, two[1], zr], zid(3)),
        )
        start([rcopy(ref, ref, out_sem.at[13], e3_r.at[i], dev) for ref, dev in moves])

    def onward_pe_in(i):
        landed(qpe.at[i, pl.ds(0, 2)], e3_r.at[i])

    first = 4
    for i in range(first):
        start(near(i, (1, 3, 2) if i < straight_steps else (1, 3)))

    more_routed.wait_recv()
    spread = dot(m0, ry[:, :, :lw].reshape(bl, lw))
    spread = jnp.where(lane // 64 == own, spread, 0.0).astype(BF16)
    fold = pick(iota((lw, 128), 0) % 64 == iota((lw, 128), 1) % 64)
    twice = dot(spread, fold)
    pairs = twice.reshape(half, 2, 16, 128)
    side = iota((half, 16, 128), 2) < 64
    qpe[:, x, z] = jnp.where(side, pairs[:, 0], pairs[:, 1]).astype(BF16)
    own_pe = twice[:, :64].astype(BF16)
    for i in range(0, first, 2):
        start(near_pe(i // 2))

    latrep[:, :lw] = dot(m1, ry[:, :, :lw].reshape(bl, lw)).astype(BF16)
    latrep[:, lw:] = dot(m1, ry[:, :, lw:].reshape(bl, 64)).astype(BF16)
    qo = qall[:, x, z].reshape(rows, lw)
    fresh = dot_nt(qo, latrep[:, :lw]) + dot_nt(own_pe, latrep[:, lw:])
    ri = iota((rows, rows), 0)
    ci = iota((rows, rows), 1)
    seen = (ri // 16 == ci // 16) & ((ci // 8) % 2 <= (ri // 8) % 2) & (ci % 8 == 0)
    fresh = jnp.where(seen, fresh * scale2, LOW)
    ftop = jnp.max(fresh, axis=1, keepdims=True)
    wf = jnp.where(seen, jnp.exp2(fresh - ftop), 0.0)
    fden = jnp.sum(wf, axis=1, keepdims=True)
    fnum = dot(wf.astype(BF16), latrep[:, :lw])

    def send(src, dst, ls, ld, n, rs, i, dev):
        return [
            rcopy(src, dst, out_sem.at[n], rs.at[0, i], dev),
            rcopy(ls, ld, out_sem.at[n + 1], rs.at[1, i], dev),
        ]

    def far(i):
        copies = []
        for j in range(2):
            a, b = pout.at[i, xo, two[j]], pout.at[half + i, two[j], zo]
            copies += send(a, h1.at[0, j, i], lrow.at[i, xo], lh1.at[0, j, i], 3, h_r, i,
                           xid(1 + 2 * j))
            copies += send(b, h1.at[1, j, i], lrow.at[half + i, zo], lh1.at[1, j, i], 3, h_r, i,
                           zid(1 + 2 * j))
        return copies

    def far_in(i):
        landed(pout.at[i, pl.ds(0, 2)], h_r.at[0, i])
        landed(lrow.at[i], h_r.at[1, i])

    last = half - 1

    def straight():
        a, b = pout.at[last, xo], pout.at[half + last, :, zo]
        return send(a, rd.at[0], lrow.at[last, xo], lrd.at[0], 3, h_r, last, xid(2)) + send(
            b, rd.at[1], lrow.at[half + last, zo], lrd.at[1], 3, h_r, last, zid(2))

    def straight_in():
        landed(rd, h_r.at[0, last])
        landed(lrd, h_r.at[1, last])

    def scatter1(i):
        copies = []
        for j in range(2):
            xt, zt = (xr, xl)[j], (zr, zl)[j]
            copies += send(pout.at[i, xt], r1.at[0, j, i], lrow.at[i, xt], lr1.at[0, j, i],
                           5, s1_r, i, xid(1 + 2 * j))
            copies += send(pout.at[half + i, :, zt], r1.at[1, j, i], lrow.at[half + i, zt],
                           lr1.at[1, j, i], 5, s1_r, i, zid(1 + 2 * j))
        return copies

    def scatter1_in(i):
        landed(pout.at[i], s1_r.at[0, i])
        landed(lrow.at[i], s1_r.at[1, i])

    def scatter2(i):
        copies = []
        for k in (1, 3, 2):
            copies += send(red1.at[0, i, lax.rem(z + k, NZ)], r2.at[0, k - 1, i], lred.at[0, i],
                           lr2.at[0, k - 1, i], 7, s2_r, i, zid(k))
            copies += send(red1.at[1, i, lax.rem(x + k, NX)], r2.at[1, k - 1, i], lred.at[1, i],
                           lr2.at[1, k - 1, i], 7, s2_r, i, xid(k))
        return copies

    def scatter2_in(i):
        landed(pout.at[i, pl.ds(0, 2), pl.ds(0, 3)], s2_r.at[0, i])
        landed(lrow.at[pl.ds(0, 2), pl.ds(0, 3)], s2_r.at[1, i])

    def weights(ls):
        top = functools.reduce(jnp.maximum, ls)
        ws = [jnp.exp2(v - top) for v in ls]
        total = functools.reduce(jnp.add, ws)
        inv = 1.0 / total
        return [w * inv for w in ws], top + jnp.log2(total)

    def column(w, n, off):
        shape = (n, 128)
        return jnp.sum(
            jnp.where(iota(shape, 1) == iota(shape, 0) + off, w, 0.0), axis=1, keepdims=True
        )

    def blend(blocks, ws, n, off):
        acc = 0.0
        for b, w in zip(blocks, ws):
            acc += column(w, n, off) * b.reshape(n, lw).astype(F32)
        return acc

    nq = 16 * NX * NZ
    row_q = iota((nq, 128), 0)
    lane_q = iota((nq, 128), 1)

    def attend(r, part):
        pltpu.make_async_copy(cache.at[r], cbuf.at[r], c_sem.at[r]).wait()
        q = qall[r].reshape(nq, lw)
        pair = qpe[r // 2].reshape(nq, 128)
        odd = jnp.full((1, 64), r % 2, F32).astype(BF16)
        pe = pair[:, :64] * (1.0 - odd) + pair[:, 64:] * odd
        c = cbuf.at[r]
        sc = dot(q, c[:lw, :]) + dot(pe, c[lw:, :])
        place = s * blk + iota((1, blk), 1)
        sc = sc + jnp.where(place < lens[g * nreq + r], 0.0, LOW)
        top = jnp.max(sc, axis=1, keepdims=True)
        w = jnp.exp2((sc - top) * scale2)
        den = jnp.sum(w, axis=1, keepdims=True)
        num = dot_nt(w.astype(BF16), c[:lw, :])
        pout[r] = (num * (1.0 / den)).astype(BF16).reshape(NX, NZ, 16, lw)
        lse = top * scale2 + jnp.log2(den)
        if part == 0:
            diag = jnp.where(lane_q == row_q % 64, lse, 0.0).reshape(4, 64, 128)
        else:
            diag = jnp.where(lane_q == row_q // 64 * 16 + row_q % 16, lse, 0.0)
            diag = jnp.sum(diag.reshape(4, 4, 16, 128), axis=0)
        for d in range(4):
            lrow[r, d] = jnp.sum(diag[d], axis=0, keepdims=True)

    lane_1 = iota((1, 128), 1)

    def middle(i):
        for j in range(2):
            xt, zt = (xr, xl)[j], (zr, zl)[j]
            keep = (lane_1 < 32) if j == 0 else (lane_1 >= 32)
            ws, ln = weights([lrow[i, xt], lh1[0, j, i]])
            acc = blend([pout[i, xt, two[j]], h1[0, j, i]], ws, 32, 32 * j)
            pout[i, xt, two[j]] = acc.astype(BF16).reshape(2, 16, lw)
            lrow[i, xt] = jnp.where(keep, ln, lrow[i, xt])
            r = half + i
            ws, ln = weights([lrow[r, zt], lh1[1, j, i]])
            acc = blend([pout[r, two[j], zt], h1[1, j, i]], ws, 32, 32 * j)
            pout[r, two[j], zt] = acc.astype(BF16).reshape(2, 16, lw)
            lrow[r, zt] = jnp.where(keep, ln, lrow[r, zt])

    def reduce1(i, more):
        ls = [lrow[i, x], lr1[0, 0, i], lr1[0, 1, i]] + ([lrd[0]] if more else [])
        blocks = [pout[i, x], r1[0, 0, i], r1[0, 1, i]] + ([rd[0]] if more else [])
        ws, ln = weights(ls)
        red1[0, i] = blend(blocks, ws, 64, 0).astype(BF16).reshape(4, 16, lw)
        lred[0, i] = ln
        r = half + i
        ls = [lrow[r, z], lr1[1, 0, i], lr1[1, 1, i]] + ([lrd[1]] if more else [])
        blocks = [pout[r, :, z], r1[1, 0, i], r1[1, 1, i]] + ([rd[1]] if more else [])
        ws, ln = weights(ls)
        red1[1, i] = blend(blocks, ws, 64, 0).astype(BF16).reshape(4, 16, lw)
        lred[1, i] = ln

    def reduce2(i):
        for part, own in ((0, z), (1, x)):
            ws, ln = weights([lred[part, i]] + [lr2[part, k, i] for k in range(3)])
            blocks = [red1[part, i, own]] + [r2[part, k, i] for k in range(3)]
            fin[part * half + i] = blend(blocks, ws, 16, own * 16)
            flse[part * half + i] = jnp.broadcast_to(column(ln, 16, own * 16), (16, 128))

    def latents(h):
        n = rows // 4
        r = half // 2
        one, other = pl.ds(r * h, r), pl.ds(half + r * h, r)
        lse = jnp.concatenate([flse[one].reshape(n, 128), flse[other].reshape(n, 128)], axis=0)
        own_num = jnp.concatenate([fin[one].reshape(n, lw), fin[other].reshape(n, lw)], axis=0)
        lse = lse[:, :1]
        high = part_of(ftop, h)
        top = jnp.maximum(high, lse)
        wc = jnp.exp2(lse - top)
        wn = jnp.exp2(high - top)
        den = wc + wn * part_of(fden, h)
        num = wc * own_num + wn * part_of(fnum, h)
        return (num * (1.0 / den)).astype(BF16)

    hrow = iota((rows // 2, 128), 0) % 8

    def project(latent, h, j):
        low = jnp.where(hrow == j, dot(latent, w_v[j]), 0.0).astype(BF16)
        high = jnp.where(hrow == j + 4, dot(latent, w_v[j + 4]), 0.0).astype(BF16)
        return dot(backs[h][0], low) + dot(backs[h][1], high)

    def step(t, carry):
        @pl.when(t + first < half)
        def _():
            start(near(t + first, (1, 3)))

        @pl.when((t + first < half) & ((t + first) % 2 == 0))
        def _():
            start(near_pe((t + first) // 2))

        @pl.when(t < straight_steps)
        def _():
            landed(qall.at[t, pl.ds(0, 2), pl.ds(0, 3)], g1_r.at[t])

        @pl.when((t >= straight_steps) & (t < half))
        def _():
            landed(qall.at[t, 0, pl.ds(0, 2)], g0_r.at[t])

        @pl.when(t < half)
        def _():
            start(direct(t))

        @pl.when(t + straight_steps < half)
        def _():
            pass_on(t + straight_steps)

        @pl.when((t < half) & (t % 2 == 0))
        def _():
            near_pe_in(t // 2)
            start(direct_pe(t // 2))

        i1 = t - 2

        @pl.when((i1 >= 0) & (i1 < half))
        def _():
            relay(i1)

        @pl.when((i1 >= 0) & (i1 < half) & (i1 % 2 == 0))
        def _():
            relay_pe(i1 // 2)

        i2 = t - 4

        @pl.when((i2 >= 0) & (i2 < half) & (i2 % 2 == 0))
        def _():
            onward_pe_in(i2 // 2)

        @pl.when((i2 >= 0) & (i2 < half))
        def _():
            onward_in(i2)
            attend(i2, 0)
            attend(half + i2, 1)

        @pl.when((i2 >= 0) & (i2 < last))
        def _():
            start(far(i2))

        @pl.when(i2 == last)
        def _():
            start(straight() + scatter1(last))

        i3 = t - 6

        @pl.when((i3 >= 0) & (i3 < last))
        def _():
            far_in(i3)
            middle(i3)
            start(scatter1(i3))

        i5 = t - 9

        @pl.when((i5 >= 0) & (i5 < last))
        def _():
            scatter1_in(i5)
            reduce1(i5, False)
            start(scatter2(i5))

        @pl.when(i5 == last)
        def _():
            scatter1_in(i5)
            straight_in()
            reduce1(i5, True)
            start(scatter2(i5))

        i7 = t - 12

        @pl.when(i7 >= 0)
        def _():
            scatter2_in(i7)
            reduce2(i7)

        @pl.when(i7 == half // 2 - 1)
        def _():
            w_copies[1].wait()
            latent = latents(0)
            for j in range(4):
                early[:, j * 128 : (j + 1) * 128] = project(latent, 0, j)

        return carry

    lax.fori_loop(0, half + 12, step, 0)

    latent = latents(1)
    for j in range(4):
        cols = pl.ds(j * 128, 128)
        back = early[:, cols] + project(latent, 1, j)
        tx2[:, :, cols] = back.astype(BF16).reshape(ngrp, 16, 128)
        if j % 2 == 1:
            part = pl.ds((j - 1) * 128, 256)
            start([
                rcopy(tx2.at[d, :, part], rx2.at[g, :, part], out_sem.at[10], rb_r.at[0], {"grp": d})
                for d in dst
            ])
    rx2[g] = tx2[g]

    def left(ref, n):
        rcopy(ref, ref, out_sem.at[n], s1_r.at[0, 0], xid(1)).wait_send()

    left(qall.at[pl.ds(0, 3)], 0)
    left(qall.at[pl.ds(0, 8)], 1)
    left(qall.at[pl.ds(0, 4)], 2)
    left(pout.at[pl.ds(0, 4)], 3)
    left(lrow.at[pl.ds(0, 10), pl.ds(0, 3)], 4)
    left(pout.at[pl.ds(0, 8)], 5)
    left(lrow.at[pl.ds(0, 8)], 6)
    left(pout.at[pl.ds(0, 3)], 7)
    left(lrow.at[pl.ds(0, 12)], 8)
    left(qpe.at[pl.ds(0, 3), :, pl.ds(0, 2)], 11)
    left(qpe.at[pl.ds(0, 4)], 12)
    left(qpe.at[pl.ds(0, 2)], 13)
    all_routed.wait_send()
    more_routed.wait_send()
    all_home = rcopy(tx2.at[most], rx2.at[most], out_sem.at[10], rb_r.at[0], gid(1))
    all_home.wait_recv()
    got = rx2[...].reshape(bl, lw)
    for f in range(2):
        for t in range(2):
            kept = dot(keeps[f][t], got)
            out[pl.ds(t * nreq, nreq), pl.ds(f * lw, lw)] = kept.astype(BF16)

    all_home.wait_send()


def on_device(
    prefill_cache, lengths, decode_slots, q_nope, q_pe, new_latent, w_uk, value_up_weight
):
    ngrp = lax.axis_size("grp")
    nreq, blk, width = prefill_cache.shape
    steps = new_latent.shape[0]
    heads, nope, lw = w_uk.shape
    half = nreq // 2
    scale2 = (nope + width - lw) ** -0.5 * LOG2E

    rows = nreq * steps * heads
    vm = pl.BlockSpec(memory_space=pltpu.VMEM)
    dma = pltpu.SemaphoreType.DMA
    bytes_in = 2 * prefill_cache.size
    out = pl.pallas_call(
        functools.partial(kernel, ngrp, nreq, blk, scale2),
        out_shape=jax.ShapeDtypeStruct((steps * nreq, heads * 128), BF16),
        in_specs=[pl.BlockSpec(memory_space=pltpu.SMEM)] + [vm] * 4
        + [pl.BlockSpec(memory_space=pl.ANY)] * 3,
        out_specs=vm,
        scratch_shapes=[
            pltpu.VMEM((nreq, width, blk), BF16),
            pltpu.VMEM((heads * nope, lw), BF16),
            pltpu.VMEM((heads, lw, 128), BF16),
            pltpu.VMEM((ngrp, 16, lw), BF16),
            pltpu.VMEM((ngrp, 16, lw), BF16),
            pltpu.VMEM((ngrp, 16, width), BF16),
            pltpu.VMEM((ngrp, 16, width), BF16),
            pltpu.VMEM((rows, width), BF16),
            pltpu.VMEM((nreq, NX, NZ, 16, lw), BF16),
            pltpu.VMEM((half, NX, NZ, 16, 128), BF16),
            pltpu.VMEM((nreq, NX, NZ, 16, lw), BF16),
            pltpu.VMEM((nreq, 4, 1, 128), F32),
            pltpu.VMEM((2, 2, half, 2, 16, lw), BF16),
            pltpu.VMEM((2, 2, half, 1, 128), F32),
            pltpu.VMEM((2, 2, half, 4, 16, lw), BF16),
            pltpu.VMEM((2, 2, half, 1, 128), F32),
            pltpu.VMEM((2, 4, 16, lw), BF16),
            pltpu.VMEM((2, 1, 128), F32),
            pltpu.VMEM((2, half, 4, 16, lw), BF16),
            pltpu.VMEM((2, half, 1, 128), F32),
            pltpu.VMEM((2, 3, half, 16, lw), BF16),
            pltpu.VMEM((2, 3, half, 1, 128), F32),
            pltpu.VMEM((nreq, 16, lw), F32),
            pltpu.VMEM((nreq, 16, 128), F32),
            pltpu.VMEM((16 * ngrp, lw), F32),
            pltpu.VMEM((ngrp, 16, lw), BF16),
            pltpu.VMEM((ngrp, 16, lw), BF16),
            dma((nreq,)), dma((2,)), dma((15,)), dma((1,)), dma((1,)), dma((1,)),
            dma((half,)), dma((half,)), dma((half,)), dma((half,)),
            dma((half // 2,)), dma((half // 2,)), dma((half // 2,)),
            dma((2, half)), dma((2, half)), dma((2, half)),
        ],
        compiler_params=pltpu.CompilerParams(
            collective_id=0, has_side_effects=True, vmem_limit_bytes=58 * 1024 * 1024
        ),
        cost_estimate=pl.CostEstimate(
            flops=2 * nreq * 256 * blk * (width + lw), bytes_accessed=bytes_in,
            transcendentals=nreq * 256 * blk,
        ),
    )(
        lengths, decode_slots,
        q_nope.reshape(steps * nreq, -1), q_pe.reshape(steps * nreq, -1),
        new_latent.reshape(steps * nreq, -1), w_uk.reshape(heads * nope, lw),
        value_up_weight, jnp.swapaxes(prefill_cache, 1, 2),
    )
    return out.reshape(steps, nreq, -1)


def solution(mesh):
    return jax.shard_map(
        on_device,
        mesh=mesh,
        in_specs=(
            P("grp", "seq", None),
            P(),
            P(),
            P(None, "grp", "seq"),
            P(None, "grp", "seq"),
            P(None, "grp", None),
            P("seq", None, None),
            P("seq", None, None),
        ),
        out_specs=P(None, "grp", "seq"),
        check_vma=False,
    )
```

```python
import functools

import jax
import jax.numpy as jnp
from jax import lax
from jax.experimental import pallas as pl
from jax.experimental.pallas import tpu as pltpu
from jax.sharding import PartitionSpec as P

MESH = pl.DeviceIdType.MESH
LOG2E = 1.4426950408889634
LOW = -1e30
CAP = 3
NX = 4
NZ = 4
F32 = jnp.float32
BF16 = jnp.bfloat16


def dot(a, b):
    return jnp.dot(a, b, preferred_element_type=F32)


def dot_nt(a, b):
    return lax.dot_general(a, b, (((1,), (1,)), ((), ())), preferred_element_type=F32)


def iota(shape, dim):
    return lax.broadcasted_iota(jnp.int32, shape, dim)


def pick(cond):
    return jnp.where(cond, 1.0, 0.0).astype(BF16)


def kernel(
    ngrp, nreq, blk, scale2,
    lens, slots, qn, qp, lat, w_uk_hbm, w_v_hbm, cache,
    out,
    cbuf, w_uk, w_v, tx, rx, ty, ry, latrep, qall, qpe, pout, lrow, h1, lh1, r1, lr1, rd, lrd, red1, lred, r2, lr2,
    fin, flse, tx2, rx2,
    c_sem, w_sem, out_sem, rt_r, ru_r, rb_r, g0_r, g1_r, g2_r, g3_r, e1_r, e2_r, e3_r, h_r, s1_r, s2_r,
):
    g = lax.axis_index("grp")
    s = lax.axis_index("seq")
    x = lax.div(s, NZ)
    z = lax.rem(s, NZ)
    half = nreq // 2
    rows = nreq * 16
    lw = 512
    c_copies = [pltpu.make_async_copy(cache.at[r], cbuf.at[r], c_sem.at[r]) for r in range(nreq)]
    w_copies = [
        pltpu.make_async_copy(w_uk_hbm, w_uk, w_sem.at[0]),
        pltpu.make_async_copy(w_v_hbm, w_v, w_sem.at[1]),
    ]
    for c in w_copies + c_copies:
        c.start()

    def gid(k):
        return {"grp": lax.rem(g + k, ngrp)}

    def xid(k):
        return {"seq": lax.rem(x + k, NX) * NZ + z}

    def zid(k):
        return {"seq": x * NZ + lax.rem(z + k, NZ)}

    def rcopy(src, dst, ss, rs, dev):
        return pltpu.make_async_remote_copy(
            src_ref=src, dst_ref=dst, send_sem=ss, recv_sem=rs, device_id=dev, device_id_type=MESH
        )

    barrier = pltpu.get_barrier_semaphore()
    for k in range(1, ngrp):
        pl.semaphore_signal(barrier, inc=1, device_id=gid(k), device_id_type=MESH)
    for k in range(1, 4):
        pl.semaphore_signal(barrier, inc=1, device_id=xid(k), device_id_type=MESH)
        pl.semaphore_signal(barrier, inc=1, device_id=zid(k), device_id_type=MESH)

    shift = nreq.bit_length() - 1
    served = slots[...]
    dest = lax.shift_right_logical(served, shift)
    lane_s = iota((ngrp, nreq), 1)
    rank = jnp.zeros((ngrp, nreq), jnp.int32)
    for j in range(nreq - 1):
        rank += jnp.where((dest == dest[:, j : j + 1]) & (lane_s > j), 1, 0)
    origin = iota((ngrp, nreq), 0) * 16 + 2 * rank
    mine = iota((ngrp, nreq), 0) == g
    rho = jnp.sum(jnp.where(mine, dest * 16 + 2 * rank, 0), axis=0, keepdims=True)
    row_id = iota((rows, nreq), 0)
    asked = g * nreq + row_id // 16
    sig = jnp.zeros((rows, nreq), jnp.int32)
    for j in range(ngrp):
        sig += jnp.where(served[j : j + 1, :] == asked, origin[j : j + 1, :], 0)
    sig = jnp.sum(sig, axis=1, keepdims=True) + (iota((rows, 1), 0) // 8) % 2

    bl = ngrp * 16
    row_l = iota((bl, nreq), 0)
    sends = [[jnp.where(row_l == rho + t + 2 * CAP * f, 1.0, 0.0) for t in range(2)] for f in range(2)]

    def send_dot(f, cols):
        both = [dot(sends[f][t].astype(BF16), cols(pl.ds(t * nreq, nreq))) for t in range(2)]
        return both[0] + both[1]

    head = send_dot(0, lambda r: qn[r, :lw]) + send_dot(1, lambda r: qn[r, lw:])
    tx[...] = head.astype(BF16).reshape(ngrp, 16, lw)
    mid = send_dot(0, lambda r: qp[r, :]) + send_dot(1, lambda r: lat[r, :lw])
    ty[:, :, :lw] = mid.astype(BF16).reshape(ngrp, 16, lw)
    tail = send_dot(1, lambda r: lat[r, lw:])
    ty[:, :, lw:] = tail.astype(BF16).reshape(ngrp, 16, 64)
    pl.semaphore_wait(barrier, ngrp - 1 + 6)
    dst = [lax.rem(g + k, ngrp) for k in range(1, ngrp)]
    route = [
        rcopy(tx.at[d], rx.at[g], out_sem.at[9], rt_r.at[0], {"grp": d}) for d in dst
    ] + [
        rcopy(ty.at[d], ry.at[g], out_sem.at[14], ru_r.at[0], {"grp": d}) for d in dst
    ]
    for c in route:
        c.start()
    rx[g] = tx[g]
    ry[g] = ty[g]
    most = pl.ds(0, ngrp - 1)
    all_routed = rcopy(tx.at[most], rx.at[most], out_sem.at[9], rt_r.at[0], gid(1))
    more_routed = rcopy(ty.at[most], ry.at[most], out_sem.at[14], ru_r.at[0], gid(1))
    all_routed.wait_recv()

    col_l = iota((rows, bl), 1)
    pulls = [jnp.where(col_l == sig + 2 * CAP * f, 1.0, 0.0) for f in range(2)]
    m0, m1 = [v.astype(BF16) for v in pulls]
    own = iota((rows, lw), 0) % 8
    lane = iota((rows, lw), 1)
    w_copies[0].wait()
    absorbed = jnp.zeros((rows, lw), F32)
    for j in range(2):
        spread = dot((m0, m1)[j], rx[...].reshape(bl, lw))
        spread = jnp.where(lane // 128 + 4 * j == own, spread, 0.0).astype(BF16)
        absorbed += dot(spread, w_uk[j * lw : (j + 1) * lw, :])
    qall[:, x, z] = absorbed.astype(BF16).reshape(nreq, 16, lw)
    xl = lax.rem(x + 3, NX)
    xr = lax.rem(x + 1, NX)
    xo = lax.rem(x + 2, NX)
    zl = lax.rem(z + 3, NZ)
    zr = lax.rem(z + 1, NZ)
    zo = lax.rem(z + 2, NZ)
    two = (pl.ds(0, 2), pl.ds(2, 2))

    def start(copies):
        for c in copies:
            c.start()

    def landed(ref, sem):
        rcopy(ref, ref, out_sem.at[0], sem, xid(1)).wait_recv()

    def near(i, hops):
        copies = []
        for k in hops:
            a, b = qall.at[i, x, z], qall.at[half + i, x, z]
            copies.append(rcopy(a, a, out_sem.at[0], g1_r.at[i], zid(k)))
            copies.append(rcopy(b, b, out_sem.at[0], g1_r.at[i], xid(k)))
        return copies

    straight_steps = 2

    def pass_on(i):
        landed(qall.at[i, 0], g1_r.at[i])
        turn = 2 * (i % 2)
        a = qall.at[i, x, lax.rem(z + 3 + turn, NZ)]
        b = qall.at[half + i, lax.rem(x + 3 + turn, NX), z]
        rcopy(a, a, out_sem.at[0], g0_r.at[i], zid(1 + turn)).start()
        rcopy(b, b, out_sem.at[0], g0_r.at[i], xid(1 + turn)).start()

    def direct(i):
        a = qall.at[i, x]
        b = qall.at[half + i, :, z]
        return [
            rcopy(ref, ref, out_sem.at[1], g2_r.at[i], dev)
            for ref, dev in ((a, xid(1)), (b, zid(1)), (a, xid(3)), (b, zid(3)))
        ]

    def direct_in(i):
        landed(qall.at[i], g2_r.at[i])

    def onward(i):
        moves = (
            (qall.at[i, xl, two[0]], xid(1)), (qall.at[half + i, two[0], zl], zid(1)),
            (qall.at[i, xr, two[1]], xid(3)), (qall.at[half + i, two[1], zr], zid(3)),
        )
        return [rcopy(ref, ref, out_sem.at[2], g3_r.at[i], dev) for ref, dev in moves]

    def onward_in(i):
        landed(qall.at[i, pl.ds(0, 2)], g3_r.at[i])

    def relay(i):
        direct_in(i)
        start(onward(i))

    quarter = half // 2

    def near_pe(i):
        copies = []
        for k in (1, 3, 2):
            a, b = qpe.at[i, x, z], qpe.at[quarter + i, x, z]
            copies.append(rcopy(a, a, out_sem.at[11], e1_r.at[i], zid(k)))
            copies.append(rcopy(b, b, out_sem.at[11], e1_r.at[i], xid(k)))
        return copies

    def near_pe_in(i):
        landed(qpe.at[i, pl.ds(0, 2), pl.ds(0, 3)], e1_r.at[i])

    def direct_pe(i):
        a = qpe.at[i, x]
        b = qpe.at[quarter + i, :, z]
        return [
            rcopy(ref, ref, out_sem.at[12], e2_r.at[i], dev)
            for ref, dev in ((a, xid(1)), (b, zid(1)), (a, xid(3)), (b, zid(3)))
        ]

    def relay_pe(i):
        landed(qpe.at[i], e2_r.at[i])
        moves = (
            (qpe.at[i, xl, two[0]], xid(1)), (qpe.at[quarter + i, two[0], zl], zid(1)),
            (qpe.at[i, xr, two[1]], xid(3)), (qpe.at[quarter + i, two[1], zr], zid(3)),
        )
        start([rcopy(ref, ref, out_sem.at[13], e3_r.at[i], dev) for ref, dev in moves])

    def onward_pe_in(i):
        landed(qpe.at[i, pl.ds(0, 2)], e3_r.at[i])

    first = 4
    for i in range(first):
        start(near(i, (1, 3, 2) if i < straight_steps else (1, 3)))

    more_routed.wait_recv()
    spread = dot(m0, ry[:, :, :lw].reshape(bl, lw))
    spread = jnp.where(lane // 64 == own, spread, 0.0).astype(BF16)
    fold = pick(iota((lw, 128), 0) % 64 == iota((lw, 128), 1) % 64)
    twice = dot(spread, fold)
    pairs = twice.reshape(half, 2, 16, 128)
    side = iota((half, 16, 128), 2) < 64
    qpe[:, x, z] = jnp.where(side, pairs[:, 0], pairs[:, 1]).astype(BF16)
    own_pe = twice[:, :64].astype(BF16)
    for i in range(0, first, 2):
        start(near_pe(i // 2))

    latrep[:, :lw] = dot(m1, ry[:, :, :lw].reshape(bl, lw)).astype(BF16)
    latrep[:, lw:] = dot(m1, ry[:, :, lw:].reshape(bl, 64)).astype(BF16)
    qo = qall[:, x, z].reshape(rows, lw)
    fresh = dot_nt(qo, latrep[:, :lw]) + dot_nt(own_pe, latrep[:, lw:])
    ri = iota((rows, rows), 0)
    ci = iota((rows, rows), 1)
    seen = (ri // 16 == ci // 16) & ((ci // 8) % 2 <= (ri // 8) % 2) & (ci % 8 == 0)
    fresh = jnp.where(seen, fresh * scale2, LOW)
    ftop = jnp.max(fresh, axis=1, keepdims=True)
    wf = jnp.where(seen, jnp.exp2(fresh - ftop), 0.0)
    fden = jnp.sum(wf, axis=1, keepdims=True)
    fnum = dot(wf.astype(BF16), latrep[:, :lw])

    def send(src, dst, ls, ld, n, rs, i, dev):
        return [
            rcopy(src, dst, out_sem.at[n], rs.at[0, i], dev),
            rcopy(ls, ld, out_sem.at[n + 1], rs.at[1, i], dev),
        ]

    def far(i):
        copies = []
        for j in range(2):
            a, b = pout.at[i, xo, two[j]], pout.at[half + i, two[j], zo]
            copies += send(a, h1.at[0, j, i], lrow.at[i, xo], lh1.at[0, j, i], 3, h_r, i,
                           xid(1 + 2 * j))
            copies += send(b, h1.at[1, j, i], lrow.at[half + i, zo], lh1.at[1, j, i], 3, h_r, i,
                           zid(1 + 2 * j))
        return copies

    def far_in(i):
        landed(pout.at[i, pl.ds(0, 2)], h_r.at[0, i])
        landed(lrow.at[i], h_r.at[1, i])

    last = half - 1

    def straight():
        a, b = pout.at[last, xo], pout.at[half + last, :, zo]
        return send(a, rd.at[0], lrow.at[last, xo], lrd.at[0], 3, h_r, last, xid(2)) + send(
            b, rd.at[1], lrow.at[half + last, zo], lrd.at[1], 3, h_r, last, zid(2))

    def straight_in():
        landed(rd, h_r.at[0, last])
        landed(lrd, h_r.at[1, last])

    def scatter1(i):
        copies = []
        for j in range(2):
            xt, zt = (xr, xl)[j], (zr, zl)[j]
            copies += send(pout.at[i, xt], r1.at[0, j, i], lrow.at[i, xt], lr1.at[0, j, i],
                           5, s1_r, i, xid(1 + 2 * j))
            copies += send(pout.at[half + i, :, zt], r1.at[1, j, i], lrow.at[half + i, zt],
                           lr1.at[1, j, i], 5, s1_r, i, zid(1 + 2 * j))
        return copies

    def scatter1_in(i):
        landed(pout.at[i], s1_r.at[0, i])
        landed(lrow.at[i], s1_r.at[1, i])

    def scatter2(i):
        copies = []
        for k in (1, 3, 2):
            copies += send(red1.at[0, i, lax.rem(z + k, NZ)], r2.at[0, k - 1, i], lred.at[0, i],
                           lr2.at[0, k - 1, i], 7, s2_r, i, zid(k))
            copies += send(red1.at[1, i, lax.rem(x + k, NX)], r2.at[1, k - 1, i], lred.at[1, i],
                           lr2.at[1, k - 1, i], 7, s2_r, i, xid(k))
        return copies

    def scatter2_in(i):
        landed(pout.at[i, pl.ds(0, 2), pl.ds(0, 3)], s2_r.at[0, i])
        landed(lrow.at[pl.ds(0, 2), pl.ds(0, 3)], s2_r.at[1, i])

    def weights(ls):
        top = functools.reduce(jnp.maximum, ls)
        ws = [jnp.exp2(v - top) for v in ls]
        total = functools.reduce(jnp.add, ws)
        inv = 1.0 / total
        return [w * inv for w in ws], top + jnp.log2(total)

    def column(w, n, off):
        shape = (n, 128)
        return jnp.sum(
            jnp.where(iota(shape, 1) == iota(shape, 0) + off, w, 0.0), axis=1, keepdims=True
        )

    def blend(blocks, ws, n, off):
        acc = 0.0
        for b, w in zip(blocks, ws):
            acc += column(w, n, off) * b.reshape(n, lw).astype(F32)
        return acc

    nq = 16 * NX * NZ
    row_q = iota((nq, 128), 0)
    lane_q = iota((nq, 128), 1)

    def attend(r, part):
        pltpu.make_async_copy(cache.at[r], cbuf.at[r], c_sem.at[r]).wait()
        q = qall[r].reshape(nq, lw)
        pair = qpe[r // 2].reshape(nq, 128)
        odd = jnp.full((1, 64), r % 2, F32).astype(BF16)
        pe = pair[:, :64] * (1.0 - odd) + pair[:, 64:] * odd
        c = cbuf.at[r]
        sc = dot(q, c[:lw, :]) + dot(pe, c[lw:, :])
        place = s * blk + iota((1, blk), 1)
        sc = sc + jnp.where(place < lens[g * nreq + r], 0.0, LOW)
        top = jnp.max(sc, axis=1, keepdims=True)
        w = jnp.exp2((sc - top) * scale2)
        den = jnp.sum(w, axis=1, keepdims=True)
        num = dot_nt(w.astype(BF16), c[:lw, :])
        pout[r] = (num * (1.0 / den)).astype(BF16).reshape(NX, NZ, 16, lw)
        lse = top * scale2 + jnp.log2(den)
        if part == 0:
            diag = jnp.where(lane_q == row_q % 64, lse, 0.0).reshape(4, 64, 128)
        else:
            diag = jnp.where(lane_q == row_q // 64 * 16 + row_q % 16, lse, 0.0)
            diag = jnp.sum(diag.reshape(4, 4, 16, 128), axis=0)
        for d in range(4):
            lrow[r, d] = jnp.sum(diag[d], axis=0, keepdims=True)

    lane_1 = iota((1, 128), 1)

    def middle(i):
        for j in range(2):
            xt, zt = (xr, xl)[j], (zr, zl)[j]
            keep = (lane_1 < 32) if j == 0 else (lane_1 >= 32)
            ws, ln = weights([lrow[i, xt], lh1[0, j, i]])
            acc = blend([pout[i, xt, two[j]], h1[0, j, i]], ws, 32, 32 * j)
            pout[i, xt, two[j]] = acc.astype(BF16).reshape(2, 16, lw)
            lrow[i, xt] = jnp.where(keep, ln, lrow[i, xt])
            r = half + i
            ws, ln = weights([lrow[r, zt], lh1[1, j, i]])
            acc = blend([pout[r, two[j], zt], h1[1, j, i]], ws, 32, 32 * j)
            pout[r, two[j], zt] = acc.astype(BF16).reshape(2, 16, lw)
            lrow[r, zt] = jnp.where(keep, ln, lrow[r, zt])

    def reduce1(i, more):
        ls = [lrow[i, x], lr1[0, 0, i], lr1[0, 1, i]] + ([lrd[0]] if more else [])
        blocks = [pout[i, x], r1[0, 0, i], r1[0, 1, i]] + ([rd[0]] if more else [])
        ws, ln = weights(ls)
        red1[0, i] = blend(blocks, ws, 64, 0).astype(BF16).reshape(4, 16, lw)
        lred[0, i] = ln
        r = half + i
        ls = [lrow[r, z], lr1[1, 0, i], lr1[1, 1, i]] + ([lrd[1]] if more else [])
        blocks = [pout[r, :, z], r1[1, 0, i], r1[1, 1, i]] + ([rd[1]] if more else [])
        ws, ln = weights(ls)
        red1[1, i] = blend(blocks, ws, 64, 0).astype(BF16).reshape(4, 16, lw)
        lred[1, i] = ln

    def reduce2(i):
        for part, own in ((0, z), (1, x)):
            ws, ln = weights([lred[part, i]] + [lr2[part, k, i] for k in range(3)])
            blocks = [red1[part, i, own]] + [r2[part, k, i] for k in range(3)]
            fin[part * half + i] = blend(blocks, ws, 16, own * 16)
            flse[part * half + i] = jnp.broadcast_to(column(ln, 16, own * 16), (16, 128))

    def of_part(copies, part):
        return [c for n, c in enumerate(copies) if n // 2 % 2 == part]

    def step(t, carry):
        @pl.when(t + first < half)
        def _():
            start(near(t + first, (1, 3)))

        @pl.when((t + first < half) & ((t + first) % 2 == 0))
        def _():
            start(near_pe((t + first) // 2))

        @pl.when(t < straight_steps)
        def _():
            landed(qall.at[t, pl.ds(0, 2), pl.ds(0, 3)], g1_r.at[t])

        @pl.when((t >= straight_steps) & (t < half))
        def _():
            landed(qall.at[t, 0, pl.ds(0, 2)], g0_r.at[t])

        @pl.when(t < half)
        def _():
            start(direct(t))

        @pl.when(t + straight_steps < half)
        def _():
            pass_on(t + straight_steps)

        @pl.when((t < half) & (t % 2 == 0))
        def _():
            near_pe_in(t // 2)
            start(direct_pe(t // 2))

        i1 = t - 2

        @pl.when((i1 >= 0) & (i1 < half))
        def _():
            relay(i1)

        @pl.when((i1 >= 0) & (i1 < half) & (i1 % 2 == 0))
        def _():
            relay_pe(i1 // 2)

        i2 = t - 4

        @pl.when((i2 >= 0) & (i2 < half) & (i2 % 2 == 0))
        def _():
            onward_pe_in(i2 // 2)

        @pl.when((i2 >= 0) & (i2 < half))
        def _():
            onward_in(i2)
            for part in range(2):
                attend(part * half + i2, part)

                @pl.when(i2 < last)
                def _():
                    start(of_part(far(i2), part))

                @pl.when(i2 == last)
                def _():
                    start(of_part(straight() + scatter1(last), part))

        i3 = t - 6

        @pl.when((i3 >= 0) & (i3 < last))
        def _():
            far_in(i3)
            middle(i3)
            start(scatter1(i3))

        i5 = t - 9

        @pl.when((i5 >= 0) & (i5 < last))
        def _():
            scatter1_in(i5)
            reduce1(i5, False)
            start(scatter2(i5))

        @pl.when(i5 == last)
        def _():
            scatter1_in(i5)
            straight_in()
            reduce1(i5, True)
            start(scatter2(i5))

        i7 = t - 12

        @pl.when(i7 >= 0)
        def _():
            scatter2_in(i7)
            reduce2(i7)

        return carry

    lax.fori_loop(0, half + 12, step, 0)

    w_copies[1].wait()
    lse = flse[...].reshape(rows, 128)[:, :1]
    top = jnp.maximum(ftop, lse)
    wc = jnp.exp2(lse - top)
    wn = jnp.exp2(ftop - top)
    den = wc + wn * fden
    num = wc * fin[...].reshape(rows, lw) + wn * fnum
    latent = (num * (1.0 / den)).astype(BF16)
    b0, b1 = [v.T.astype(BF16) for v in pulls]
    hrow = iota((rows, 128), 0) % 8
    for j in range(4):
        va0 = jnp.where(hrow == j, dot(latent, w_v[j]), 0.0).astype(BF16)
        vb0 = jnp.where(hrow == j + 4, dot(latent, w_v[j + 4]), 0.0).astype(BF16)
        back = dot(b0, va0) + dot(b1, vb0)
        tx2[:, :, j * 128 : (j + 1) * 128] = back.astype(BF16).reshape(ngrp, 16, 128)
        if j % 2 == 1:
            part = pl.ds((j - 1) * 128, 256)
            start([
                rcopy(tx2.at[d, :, part], rx2.at[g, :, part], out_sem.at[10], rb_r.at[0], {"grp": d})
                for d in dst
            ])

    rx2[g] = tx2[g]

    def left(ref, n):
        rcopy(ref, ref, out_sem.at[n], s1_r.at[0, 0], xid(1)).wait_send()

    left(qall.at[pl.ds(0, 3)], 0)
    left(qall.at[pl.ds(0, 8)], 1)
    left(qall.at[pl.ds(0, 4)], 2)
    left(pout.at[pl.ds(0, 4)], 3)
    left(lrow.at[pl.ds(0, 10), pl.ds(0, 3)], 4)
    left(pout.at[pl.ds(0, 8)], 5)
    left(lrow.at[pl.ds(0, 8)], 6)
    left(pout.at[pl.ds(0, 3)], 7)
    left(lrow.at[pl.ds(0, 12)], 8)
    left(qpe.at[pl.ds(0, 3), :, pl.ds(0, 2)], 11)
    left(qpe.at[pl.ds(0, 4)], 12)
    left(qpe.at[pl.ds(0, 2)], 13)
    all_routed.wait_send()
    more_routed.wait_send()
    all_home = rcopy(tx2.at[most], rx2.at[most], out_sem.at[10], rb_r.at[0], gid(1))
    all_home.wait_recv()
    got = rx2[...].reshape(bl, lw)
    for f in range(2):
        for t in range(2):
            kept = dot(sends[f][t].T.astype(BF16), got)
            out[pl.ds(t * nreq, nreq), pl.ds(f * lw, lw)] = kept.astype(BF16)

    all_home.wait_send()


def on_device(
    prefill_cache, lengths, decode_slots, q_nope, q_pe, new_latent, w_uk, value_up_weight
):
    ngrp = lax.axis_size("grp")
    nreq, blk, width = prefill_cache.shape
    steps = new_latent.shape[0]
    heads, nope, lw = w_uk.shape
    half = nreq // 2
    scale2 = (nope + width - lw) ** -0.5 * LOG2E

    rows = nreq * steps * heads
    vm = pl.BlockSpec(memory_space=pltpu.VMEM)
    dma = pltpu.SemaphoreType.DMA
    bytes_in = 2 * prefill_cache.size
    out = pl.pallas_call(
        functools.partial(kernel, ngrp, nreq, blk, scale2),
        out_shape=jax.ShapeDtypeStruct((steps * nreq, heads * 128), BF16),
        in_specs=[pl.BlockSpec(memory_space=pltpu.SMEM)] + [vm] * 4
        + [pl.BlockSpec(memory_space=pl.ANY)] * 3,
        out_specs=vm,
        scratch_shapes=[
            pltpu.VMEM((nreq, width, blk), BF16),
            pltpu.VMEM((heads * nope, lw), BF16),
            pltpu.VMEM((heads, lw, 128), BF16),
            pltpu.VMEM((ngrp, 16, lw), BF16),
            pltpu.VMEM((ngrp, 16, lw), BF16),
            pltpu.VMEM((ngrp, 16, width), BF16),
            pltpu.VMEM((ngrp, 16, width), BF16),
            pltpu.VMEM((rows, width), BF16),
            pltpu.VMEM((nreq, NX, NZ, 16, lw), BF16),
            pltpu.VMEM((half, NX, NZ, 16, 128), BF16),
            pltpu.VMEM((nreq, NX, NZ, 16, lw), BF16),
            pltpu.VMEM((nreq, 4, 1, 128), F32),
            pltpu.VMEM((2, 2, half, 2, 16, lw), BF16),
            pltpu.VMEM((2, 2, half, 1, 128), F32),
            pltpu.VMEM((2, 2, half, 4, 16, lw), BF16),
            pltpu.VMEM((2, 2, half, 1, 128), F32),
            pltpu.VMEM((2, 4, 16, lw), BF16),
            pltpu.VMEM((2, 1, 128), F32),
            pltpu.VMEM((2, half, 4, 16, lw), BF16),
            pltpu.VMEM((2, half, 1, 128), F32),
            pltpu.VMEM((2, 3, half, 16, lw), BF16),
            pltpu.VMEM((2, 3, half, 1, 128), F32),
            pltpu.VMEM((nreq, 16, lw), F32),
            pltpu.VMEM((nreq, 16, 128), F32),
            pltpu.VMEM((ngrp, 16, lw), BF16),
            pltpu.VMEM((ngrp, 16, lw), BF16),
            dma((nreq,)), dma((2,)), dma((15,)), dma((1,)), dma((1,)), dma((1,)),
            dma((half,)), dma((half,)), dma((half,)), dma((half,)),
            dma((half // 2,)), dma((half // 2,)), dma((half // 2,)),
            dma((2, half)), dma((2, half)), dma((2, half)),
        ],
        compiler_params=pltpu.CompilerParams(
            collective_id=0, has_side_effects=True, vmem_limit_bytes=58 * 1024 * 1024
        ),
        cost_estimate=pl.CostEstimate(
            flops=2 * nreq * 256 * blk * (width + lw), bytes_accessed=bytes_in,
            transcendentals=nreq * 256 * blk,
        ),
    )(
        lengths, decode_slots,
        q_nope.reshape(steps * nreq, -1), q_pe.reshape(steps * nreq, -1),
        new_latent.reshape(steps * nreq, -1), w_uk.reshape(heads * nope, lw),
        value_up_weight, jnp.swapaxes(prefill_cache, 1, 2),
    )
    return out.reshape(steps, nreq, -1)


def solution(mesh):
    return jax.shard_map(
        on_device,
        mesh=mesh,
        in_specs=(
            P("grp", "seq", None),
            P(),
            P(),
            P(None, "grp", "seq"),
            P(None, "grp", "seq"),
            P(None, "grp", None),
            P("seq", None, None),
            P("seq", None, None),
        ),
        out_specs=P(None, "grp", "seq"),
        check_vma=False,
    )
```
